32 devices in a mesh: row: 16 (over z, x, core), col: 2 (over y).
Axes of the slice: x: 2, y: 2, z: 4, core: 2. Of those that a mesh axis runs over, the one named last changes fastest.
Arguments:
- c_panel: float32 [8192, 128], P('row', 'col'), may hold values from -0.0625 to 0.0625
- cbar_in: float32 [8192, 128], P('row', 'col'), may hold values from -6 to 6
- factor_diagonal_block: float32 [128, 128], replicated, may hold values from -0.9 to 4, as said below
- dbar_in: float32 [128, 128], replicated, may hold values from -6 to 6
- r_panel: float32 [128, 4096], P('row', 'col'), may hold values from -0.6 to 0.6
- rbar_in: float32 [128, 4096], P('row', 'col'), may hold values from -6 to 6
- b_block: float32 [8192, 4096], P('row', 'col'), may hold values from -0.0625 to 0.0625
- bbar_in: float32 [8192, 4096], P('row', 'col'), may hold values from -6 to 6
Outputs:
- cbar_out: float32 [8192, 128], P('row', 'col')
- bbar_out: float32 [8192, 4096], P('row', 'col')
- kernel_diagonal_adjoint: float32 [128, 128], P('row', 'col')
- rbar_out: float32 [128, 4096], P('row', 'col')
The draws below stay inside these ranges and needn't reach their ends.
Inputs may be any that keep to these rules, and one draw needn't show every extreme that they name: factor_diagonal_block is lower triangular; its diagonal entries lie in 2 to 4 and its entries below the diagonal in -0.9 to 0.9.
All inputs are finite; a program needn't handle non-finite values.
Results may differ from the reference program's by a relative error of at most 0.00007.
Values sent between devices are 32-bit elements; how exact they have to be, the bound alone decides.
No kernel may reach another device: no remote copies, remote signals or barrier semaphores. Data moves between devices by JAX's collectives and lax.ppermute only.
A program may use at most 64 MiB of HBM per device.

```python
import jax
import jax.numpy as jnp
from jax import lax

NB = 128
M = 8192
J = 4096


def draw_factor_diagonal_block(key, part):
    key = jax.random.fold_in(key, 7)
    first, second = jax.random.split(key)
    diag_vals = jax.random.uniform(first, (NB,), jnp.float32, 2.0, 4.0)
    lower_vals = jnp.clip(jax.random.normal(second, (NB, NB), jnp.float32) * 0.15, -0.9, 0.9)
    return jnp.tril(lower_vals, -1) + jnp.diag(diag_vals)


def level_of(key, dims, cuts, smallest, top_value):
    def one(position, parts):
        steps = jax.random.uniform(jax.random.fold_in(jax.random.fold_in(key, 6), position), (parts,), jnp.float32, smallest / len(cuts), top_value / len(cuts))
        return jnp.repeat(jnp.exp(steps), dims[position] // parts).reshape((-1,) + (1,) * (len(dims) - position - 1))

    loudness = one(*cuts[0])
    for cut in cuts[1:]:
        loudness = loudness * one(*cut)
    return loudness


def gaussian(key, shape, width, limit, pieces=(), kind=jnp.bfloat16):
    loudness = level_of(key, shape, pieces, -0.22, 0.18) if pieces else 1.0
    result = jax.random.normal(key, shape, jnp.float32) * width * loudness
    return jnp.minimum(jnp.maximum(result, -limit), limit).astype(kind)


def setup_inputs(seed: int = 0) -> dict:
    keys = jax.random.split(jax.random.key(seed), 9)
    return {
        "c_panel": gaussian(keys[0], (M, NB), M ** -0.5, 0.0625, ((0, 16), (1, 2)), jnp.float32),
        "cbar_in": gaussian(keys[1], (M, NB), 1.0, 6.0, ((0, 16), (1, 2)), jnp.float32),
        "factor_diagonal_block": draw_factor_diagonal_block(jax.random.fold_in(keys[8], 71), 0),
        "dbar_in": gaussian(keys[3], (NB, NB), 1.0, 6.0, (), jnp.float32),
        "r_panel": gaussian(keys[4], (NB, J), 0.1, 0.6, ((0, 16), (1, 2)), jnp.float32),
        "rbar_in": gaussian(keys[5], (NB, J), 1.0, 6.0, ((0, 16), (1, 2)), jnp.float32),
        "b_block": gaussian(keys[6], (M, J), M ** -0.5, 0.0625, ((0, 16), (1, 2)), jnp.float32),
        "bbar_in": gaussian(keys[7], (M, J), 1.0, 6.0, ((0, 16), (1, 2)), jnp.float32),
    }


def lower_half_term(matrix):
    return jnp.tril(matrix) - 0.5 * jnp.diag(jnp.diag(matrix))

def reference(c_panel, cbar_in, factor_diagonal_block, dbar_in, r_panel, rbar_in, b_block, bbar_in):
    highest = lax.Precision.HIGHEST
    cbar_out = jax.scipy.linalg.solve_triangular(factor_diagonal_block, cbar_in.T, lower=True, trans='T').T
    bbar_out = bbar_in - jnp.dot(cbar_out.astype(jnp.float32), r_panel.astype(jnp.float32), precision=highest, preferred_element_type=jnp.float32)
    diagonal_adjoint_middle = dbar_in - jnp.tril(jnp.dot(cbar_out.T.astype(jnp.float32), c_panel.astype(jnp.float32), precision=highest, preferred_element_type=jnp.float32))
    proj = lower_half_term(jnp.dot(factor_diagonal_block.T.astype(jnp.float32), diagonal_adjoint_middle.astype(jnp.float32), precision=highest, preferred_element_type=jnp.float32))
    left_product_term = jax.scipy.linalg.solve_triangular(factor_diagonal_block, proj, lower=True, trans='T')
    sandwich_product = jax.scipy.linalg.solve_triangular(factor_diagonal_block, left_product_term.T, lower=True, trans='T').T
    kernel_diagonal_adjoint = lower_half_term(sandwich_product + sandwich_product.T)
    rbar_out = rbar_in - jnp.dot(cbar_out.T.astype(jnp.float32), b_block.astype(jnp.float32), precision=highest, preferred_element_type=jnp.float32)
    rbar_out = rbar_out - jnp.dot((kernel_diagonal_adjoint + kernel_diagonal_adjoint.T).astype(jnp.float32), r_panel.astype(jnp.float32), precision=highest, preferred_element_type=jnp.float32)
    return (cbar_out, bbar_out, kernel_diagonal_adjoint, rbar_out)
```

```python
import jax
import jax.numpy as jnp
from jax import lax
from jax.experimental import pallas as pl
from jax.experimental.pallas import tpu as pltpu
from jax.sharding import PartitionSpec as P

HIGHEST = lax.Precision.HIGHEST
HIGH = lax.Precision.HIGH
F32 = jnp.float32
BF16 = jnp.bfloat16
MIB = 1 << 20
LANES = 128


def dot(a, b, dims=((1,), (0,)), precision=HIGHEST):
    return lax.dot_general(a, b, (dims, ((), ())), precision=precision, preferred_element_type=F32)


def iotas(shape):
    return lax.broadcasted_iota(jnp.int32, shape, 0), lax.broadcasted_iota(jnp.int32, shape, 1)


def phi(matrix):
    i, j = iotas(matrix.shape)
    return jnp.where(i > j, matrix, jnp.where(i == j, 0.5 * matrix, 0.0))


def split(value):
    high = value.astype(BF16)
    return high, (value - high.astype(F32)).astype(BF16)


def hot(cond):
    return jnp.where(cond, 1.0, 0.0).astype(F32)


def swap(value, axis, size, offset):
    return lax.ppermute(value, axis, [(i, i ^ offset) for i in range(size)])


def full(shape, dtype=F32):
    return jax.ShapeDtypeStruct(shape, dtype)


class Grid:
    def __init__(self, rows, cols, height, width):
        self.rows, self.cols, self.height, self.width = rows, cols, height, width
        cores, zs = 2, 4
        xs = rows // (cores * zs)
        self.core, self.x, self.z = (cores, 1), (xs, cores), (zs, xs * cores)
        self.z_near, self.z_far = (2, xs * cores), (2, 2 * xs * cores)
        self.order = (self.core, self.x, self.z)

    def offsets(self):
        found = [0]
        for count, stride in self.order:
            found = [base + d * stride for base in found for d in range(count)]
        return found

    def relative_row(self, position, me):
        block, inner = position // self.height, position % self.height
        offset = jnp.zeros_like(block)
        for count, stride in self.order[::-1]:
            offset = offset + (block % count) * stride
            block = block // count
        return (offset ^ me) * self.height + inner

    def permute_rows(self, ref, me):
        n, h = ref.shape[0], self.height
        if h % 8 == 0:
            return jnp.concatenate(
                [ref[pl.ds(pl.multiple_of((offset ^ me) * h, h), h), :] for offset in self.offsets()], axis=0
            )
        i, j = iotas((n, n))
        return dot(hot(j == self.relative_row(i, me)), ref[...])


def prepare_kernel(factor_ref, b_hbm, inverse_ref, high_ref, low_ref, b_ref, sems):
    chunks = sems.shape[0]
    step = b_ref.shape[0] // chunks
    copies = [
        pltpu.make_async_copy(b_hbm.at[pl.ds(k * step, step)], b_ref.at[pl.ds(k * step, step)], sems.at[k])
        for k in range(chunks)
    ]
    for copy in copies:
        copy.start()

    def split_chunk(k):
        copies[k].wait()
        at = slice(k * step, (k + 1) * step)
        high_ref[at, :], low_ref[at, :] = split(b_ref[at, :])

    factor = factor_ref[...]
    n = factor.shape[0]
    i, j = iotas((n, n))
    diagonal = jnp.where(i == j, factor, 0.0)
    recip_row = 1.0 / jnp.sum(diagonal, axis=0, keepdims=True)
    recip_col = 1.0 / jnp.sum(diagonal, axis=1, keepdims=True)
    size, level = 1, 0
    while size < n:
        below = (i // (2 * size) == j // (2 * size)) & ((i // size) % 2 == 1) & ((j // size) % 2 == 0)
        block = jnp.where(below, factor, 0.0)
        if level == 0:
            inverse = jnp.where(i == j, recip_row, -(recip_col * block * recip_row))
        else:
            inverse = inverse - dot(dot(inverse, block), inverse)
        if 2 <= level < 2 + chunks:
            split_chunk(level - 2)
        size, level = 2 * size, level + 1
    inverse_ref[...] = inverse
    for k in range(max(level - 2, 0), chunks):
        split_chunk(k)


def fold(matrix):
    n = matrix.shape[0]
    m = n // 2
    i, j = iotas((m, m))
    corner = matrix[m:, m:]
    mixed = jnp.where(i >= j, matrix[:m, :m], corner.T)
    diagonal = jnp.sum(jnp.where(i == j, corner, 0.0), axis=0, keepdims=True)
    top = jnp.concatenate([matrix[m:, :m], mixed], axis=1)
    last = jnp.broadcast_to(jnp.concatenate([diagonal, diagonal], axis=1), (8, n))
    return jnp.concatenate([top[k:k + 8] for k in range(0, m, 8)] + [last], axis=1)


def unfold(folded, n):
    folded = jnp.concatenate([folded[:, k:k + n] for k in range(0, folded.shape[1], n)], axis=0)
    m = n // 2
    i, j = iotas((m, m))
    mixed = folded[:m, m:]
    corner = jnp.where(i == j, folded[m:m + 1, :m], jnp.where(i > j, mixed.T, 0.0))
    upper = jnp.concatenate([jnp.where(i >= j, mixed, 0.0), jnp.zeros((m, m), F32)], axis=1)
    return jnp.concatenate([upper, jnp.concatenate([folded[:m, :m], corner], axis=1)], axis=0)


def cbar_kernel(grid, inverse_ref, *refs):
    cols = grid.cols
    cbar_refs, c_refs = refs[:cols], refs[cols:2 * cols]
    out_ref, product_ref, perm_ref, stack_ref, cbar, c, new = refs[2 * cols:]
    me, my_col = lax.axis_index("row"), lax.axis_index("col")
    n = inverse_ref.shape[0]
    for d in range(cols):
        at = pl.ds(pl.multiple_of((my_col ^ d) * grid.width, grid.width), grid.width)
        cbar[at, :] = cbar_refs[d][...]
        c[at, :] = c_refs[d][...]
    absolute = dot(inverse_ref[...].T, cbar[...])
    new[...] = absolute
    perm = grid.permute_rows(new, me)
    perm_ref[...] = perm
    stack_ref[:n, :], stack_ref[n:, :] = split(perm)
    out_ref[...] = new[pl.ds(pl.multiple_of(my_col * grid.width, grid.width), grid.width), :]
    product_ref[...] = fold(dot(absolute, c[...], ((1,), (1,))))


def trailing_kernel(stack_ref, high_ref, low_ref, keep_ref, send_ref):
    n = stack_ref.shape[0] // 2
    breadth = high_ref.shape[1]
    tile = 256
    for k in range(breadth // tile):
        at = slice(k * tile, (k + 1) * tile)
        stacked = dot(stack_ref[...], high_ref[:, at], precision=None)
        total = stacked[:n] + stacked[n:] + dot(stack_ref[:n, :], low_ref[:, at], precision=None)
        keep_ref[:, at] = total[:n // 2]
        send_ref[:, at] = total[n // 2:]


def bbar_kernel(perm_ref, sym_ref, panel_ref, bbar_ref, rbar_ref, out_hbm, rbar_out_ref, out_ref, left_ref, sems):
    n, depth = perm_ref.shape
    height = sym_ref.shape[0]
    left_ref[:depth, :n], left_ref[:depth, n:] = split(perm_ref[...].T)
    sym = jnp.concatenate([sym_ref[...], jnp.zeros((16 - height, n), F32)], axis=0)
    left_ref[depth:, :n], left_ref[depth:, n:] = split(sym)
    count = sems.shape[0]
    tile = panel_ref.shape[1] // count
    copies = []
    for k in range(count):
        at = slice(k * tile, (k + 1) * tile)
        high, low = split(panel_ref[:, at])
        update = dot(left_ref[...], jnp.concatenate([high, high], axis=0), precision=None)
        update = update + dot(left_ref[:, :n], low, precision=None)
        out_ref[:, at] = bbar_ref[:, at] - update[:depth]
        rbar_out_ref[:, at] = rbar_ref[:, at] - update[depth:depth + height]
        copies.append(pltpu.make_async_copy(out_ref.at[:, pl.ds(k * tile, tile)], out_hbm.at[:, pl.ds(k * tile, tile)], sems.at[k]))
        copies[-1].start()
    for copy in copies:
        copy.wait()


def diagonal_kernel(grid, factor_ref, inverse_ref, dbar_ref, *refs):
    products, (out_ref, sym_ref) = refs[:-2], refs[-2:]
    me, my_col = lax.axis_index("row"), lax.axis_index("col")
    n, height, width = factor_ref.shape[0], grid.height, grid.width
    i, j = iotas((n, n))
    inverse = inverse_ref[...]
    si, sj = iotas((height, n))
    own_row = me * height + si
    weights = dot(hot(sj == own_row), inverse.T)
    inverse_perm = dot(inverse, hot(i == grid.relative_row(j, me)))
    product = unfold(add_pairs([ref[...] for ref in products]), n)
    proj = phi(dot(factor_ref[...].T, dbar_ref[...] - product))
    half = dot(weights, proj + proj.T)
    rows_sym = dot(half, inverse)
    sym_ref[...] = dot(half, inverse_perm)
    rows_kernel = jnp.where(sj < own_row, rows_sym, jnp.where(sj == own_row, 0.5 * rows_sym, 0.0))
    ci, cj = iotas((n, width))
    out_ref[...] = dot(rows_kernel, hot(ci == my_col * width + cj))


def call(kernel, out_shape, scratch=(), limit=8 * MIB, flops=0, specs=None):
    return pl.pallas_call(
        kernel,
        out_shape=out_shape,
        scratch_shapes=list(scratch),
        compiler_params=pltpu.CompilerParams(vmem_limit_bytes=limit),
        cost_estimate=pl.CostEstimate(flops=flops, bytes_accessed=1, transcendentals=0),
        **({"in_specs": specs} if specs else {}),
    )


def add_pairs(terms):
    while len(terms) > 1:
        terms = [a + b for a, b in zip(terms[::2], terms[1::2])]
    return terms[0]


def make_body(rows, cols):
    def row_parts(value, step):
        count, stride = step
        return [value] + [swap(value, "row", rows, d * stride) for d in range(1, count)]

    def col_parts(value):
        return [value] + [swap(value, "col", cols, d) for d in range(1, cols)]

    def body(c_panel, cbar_in, factor, dbar_in, r_panel, rbar_in, b_block, bbar_in):
        n = factor.shape[0]
        depth, width = c_panel.shape
        height, breadth = r_panel.shape
        grid = Grid(rows, cols, height, width)

        cbar_parts, c_parts = col_parts(cbar_in.T), col_parts(c_panel.T)
        panel = jnp.concatenate(row_parts(r_panel, grid.z), axis=0)
        panel = jnp.concatenate(row_parts(panel, grid.x), axis=0)

        inverse, high, low = call(
            prepare_kernel,
            (full((n, n)), full((depth, breadth), BF16), full((depth, breadth), BF16)),
            [pltpu.VMEM((depth, breadth), F32), pltpu.SemaphoreType.DMA((8,))],
            limit=48 * MIB, flops=4 * 10 ** 9,
            specs=[pl.BlockSpec(memory_space=pltpu.VMEM), pl.BlockSpec(memory_space=pltpu.HBM)],
        )(factor, b_block)
        cbar_out_t, product, cbar_perm, stack = call(
            lambda *refs: cbar_kernel(grid, *refs),
            (full((width, depth)), full((8, (n // 16 + 1) * n)), full((n, depth)), full((2 * n, depth), BF16)),
            [pltpu.VMEM((n, depth), F32)] * 3, flops=10 ** 9,
        )(inverse, *cbar_parts, *c_parts)

        keep, send = call(trailing_kernel, (full((n // 2, breadth)),) * 2, flops=10 ** 9)(stack, high, low)
        summed = keep + swap(send, "row", rows, grid.core[1])
        product = add_pairs(row_parts(product, grid.z_near))
        product, summed = lax.optimization_barrier((product, summed))
        product = add_pairs(row_parts(product, grid.core))
        product, panel = lax.optimization_barrier((product, panel))
        panel = jnp.concatenate(row_parts(panel, grid.core), axis=0)
        product = add_pairs(row_parts(product, grid.z_far))
        product_parts = row_parts(product, grid.x)
        for count, stride in grid.order[1:]:
            blocks = summed.reshape(count, -1, breadth)
            summed = add_pairs([blocks[0]] + [swap(blocks[d], "row", rows, d * stride) for d in range(1, count)])
            if stride == grid.x[1]:
                summed, dbar_in = lax.optimization_barrier((summed, dbar_in))
        kernel_out, sym = call(
            lambda *refs: diagonal_kernel(grid, *refs), (full((height, width)), full((height, n)))
        )(factor, inverse, dbar_in, *product_parts)
        vmem = pl.BlockSpec(memory_space=pltpu.VMEM)
        bbar_out, rbar = pl.pallas_call(
            bbar_kernel,
            in_specs=[vmem] * 5,
            out_specs=[pl.BlockSpec(memory_space=pltpu.HBM), vmem],
            out_shape=(full((depth, breadth)), full((height, breadth))),
            scratch_shapes=[
                pltpu.VMEM((depth, breadth), F32), pltpu.VMEM((depth + 16, 2 * n), BF16), pltpu.SemaphoreType.DMA((breadth // 256,))
            ],
            compiler_params=pltpu.CompilerParams(vmem_limit_bytes=16 * MIB),
            cost_estimate=pl.CostEstimate(flops=10 ** 9, bytes_accessed=1, transcendentals=0),
        )(cbar_perm, sym, panel, bbar_in, rbar_in)
        return (cbar_out_t.T, bbar_out, kernel_out, rbar - summed)

    return body


def solution(mesh):
    spec = P("row", "col")
    in_specs = (spec, spec, P(), P(), spec, spec, spec, spec)
    return jax.shard_map(
        make_body(mesh.shape["row"], mesh.shape["col"]),
        mesh=mesh, in_specs=in_specs, out_specs=(spec,) * 4, check_vma=False,
    )
```

```python
import jax
import jax.numpy as jnp
from jax import lax
from jax.experimental import pallas as pl
from jax.experimental.pallas import tpu as pltpu
from jax.sharding import PartitionSpec as P

HIGHEST = lax.Precision.HIGHEST
HIGH = lax.Precision.HIGH
F32 = jnp.float32
BF16 = jnp.bfloat16
MIB = 1 << 20
LANES = 128


def dot(a, b, dims=((1,), (0,)), precision=HIGHEST):
    return lax.dot_general(a, b, (dims, ((), ())), precision=precision, preferred_element_type=F32)


def iotas(shape):
    return lax.broadcasted_iota(jnp.int32, shape, 0), lax.broadcasted_iota(jnp.int32, shape, 1)


def phi(matrix):
    i, j = iotas(matrix.shape)
    return jnp.where(i > j, matrix, jnp.where(i == j, 0.5 * matrix, 0.0))


def split(value):
    high = value.astype(BF16)
    return high, (value - high.astype(F32)).astype(BF16)


def hot(cond):
    return jnp.where(cond, 1.0, 0.0).astype(F32)


def swap(value, axis, size, offset):
    return lax.ppermute(value, axis, [(i, i ^ offset) for i in range(size)])


def full(shape, dtype=F32):
    return jax.ShapeDtypeStruct(shape, dtype)


class Grid:
    def __init__(self, rows, cols, height, width):
        self.rows, self.cols, self.height, self.width = rows, cols, height, width
        cores, zs = 2, 4
        xs = rows // (cores * zs)
        self.core, self.x, self.z = (cores, 1), (xs, cores), (zs, xs * cores)
        self.z_near, self.z_far = (2, xs * cores), (2, 2 * xs * cores)
        self.order = (self.core, self.x, self.z)

    def offsets(self):
        found = [0]
        for count, stride in self.order:
            found = [base + d * stride for base in found for d in range(count)]
        return found

    def relative_row(self, position, me):
        block, inner = position // self.height, position % self.height
        offset = jnp.zeros_like(block)
        for count, stride in self.order[::-1]:
            offset = offset + (block % count) * stride
            block = block // count
        return (offset ^ me) * self.height + inner

    def permute_rows(self, ref, me):
        n, h = ref.shape[0], self.height
        if h % 8 == 0:
            return jnp.concatenate(
                [ref[pl.ds(pl.multiple_of((offset ^ me) * h, h), h), :] for offset in self.offsets()], axis=0
            )
        i, j = iotas((n, n))
        return dot(hot(j == self.relative_row(i, me)), ref[...])


def identity_kernel(out_ref):
    i, j = iotas(out_ref.shape)
    out_ref[...] = hot(i == j)


def prepare_kernel(factor_ref, identity_ref, b_hbm, inverse_ref, high_ref, low_ref, b_ref, sems):
    chunks = sems.shape[0]
    step = b_ref.shape[0] // chunks
    copies = [
        pltpu.make_async_copy(b_hbm.at[pl.ds(k * step, step)], b_ref.at[pl.ds(k * step, step)], sems.at[k])
        for k in range(chunks)
    ]
    for copy in copies:
        copy.start()

    def split_chunk(k):
        copies[k].wait()
        at = slice(k * step, (k + 1) * step)
        high_ref[at, :], low_ref[at, :] = split(b_ref[at, :])

    factor = factor_ref[...]
    n = factor.shape[0]
    i, j = iotas((n, n))
    diagonal = factor * identity_ref[...]
    recip_row = 1.0 / jnp.sum(diagonal, axis=0, keepdims=True)
    recip_col = 1.0 / jnp.sum(diagonal, axis=1, keepdims=True)
    size, level = 1, 0
    while size < n:
        below = (i // (2 * size) == j // (2 * size)) & ((i // size) % 2 == 1) & ((j // size) % 2 == 0)
        block = jnp.where(below, factor, 0.0)
        if level == 0:
            inverse = jnp.where(i == j, recip_row, -(recip_col * block * recip_row))
        else:
            inverse = inverse - dot(dot(inverse, block), inverse)
        if 2 <= level < 2 + chunks:
            split_chunk(level - 2)
        size, level = 2 * size, level + 1
    inverse_ref[...] = inverse
    for k in range(max(level - 2, 0), chunks):
        split_chunk(k)


def fold(matrix):
    n = matrix.shape[0]
    m = n // 2
    i, j = iotas((m, m))
    corner = matrix[m:, m:]
    mixed = jnp.where(i >= j, matrix[:m, :m], corner.T)
    diagonal = jnp.sum(jnp.where(i == j, corner, 0.0), axis=0, keepdims=True)
    top = jnp.concatenate([matrix[m:, :m], mixed], axis=1)
    last = jnp.broadcast_to(jnp.concatenate([diagonal, diagonal], axis=1), (8, n))
    return jnp.concatenate([top[k:k + 8] for k in range(0, m, 8)] + [last], axis=1)


def unfold(folded, n):
    folded = jnp.concatenate([folded[:, k:k + n] for k in range(0, folded.shape[1], n)], axis=0)
    m = n // 2
    i, j = iotas((m, m))
    mixed = folded[:m, m:]
    corner = jnp.where(i == j, folded[m:m + 1, :m], jnp.where(i > j, mixed.T, 0.0))
    upper = jnp.concatenate([jnp.where(i >= j, mixed, 0.0), jnp.zeros((m, m), F32)], axis=1)
    return jnp.concatenate([upper, jnp.concatenate([folded[:m, :m], corner], axis=1)], axis=0)


def cbar_kernel(grid, inverse_ref, *refs):
    cols = grid.cols
    cbar_refs, c_refs = refs[:cols], refs[cols:2 * cols]
    out_ref, product_ref, perm_ref, stack_ref, cbar, c, new = refs[2 * cols:]
    me, my_col = lax.axis_index("row"), lax.axis_index("col")
    n = inverse_ref.shape[0]
    for d in range(cols):
        at = pl.ds(pl.multiple_of((my_col ^ d) * grid.width, grid.width), grid.width)
        cbar[at, :] = cbar_refs[d][...]
        c[at, :] = c_refs[d][...]
    absolute = dot(inverse_ref[...].T, cbar[...])
    new[...] = absolute
    perm = grid.permute_rows(new, me)
    perm_ref[...] = perm
    stack_ref[:n, :], stack_ref[n:, :] = split(perm)
    out_ref[...] = new[pl.ds(pl.multiple_of(my_col * grid.width, grid.width), grid.width), :]
    product_ref[...] = fold(dot(absolute, c[...], ((1,), (1,))))


def trailing_kernel(stack_ref, high_ref, low_ref, keep_ref, send_ref):
    n = stack_ref.shape[0] // 2
    breadth = high_ref.shape[1]
    tile = 256
    for k in range(breadth // tile):
        at = slice(k * tile, (k + 1) * tile)
        stacked = dot(stack_ref[...], high_ref[:, at], precision=None)
        total = stacked[:n] + stacked[n:] + dot(stack_ref[:n, :], low_ref[:, at], precision=None)
        keep_ref[:, at] = total[:n // 2]
        send_ref[:, at] = total[n // 2:]


def bbar_kernel(perm_ref, bbar_ref, *refs):
    panel_refs, (out_hbm, out_ref, left_ref, sems) = refs[:-4], refs[-4:]
    n = perm_ref.shape[0]
    left_ref[:, :n], left_ref[:, n:] = split(perm_ref[...].T)
    count = sems.shape[0]
    tile = bbar_ref.shape[1] // count
    copies = []
    for k in range(count):
        at = slice(k * tile, (k + 1) * tile)
        high, low = split(jnp.concatenate([ref[:, at] for ref in panel_refs], axis=0))
        update = dot(left_ref[...], jnp.concatenate([high, high], axis=0), precision=None)
        out_ref[:, at] = bbar_ref[:, at] - (update + dot(left_ref[:, :n], low, precision=None))
        copies.append(pltpu.make_async_copy(out_ref.at[:, pl.ds(k * tile, tile)], out_hbm.at[:, pl.ds(k * tile, tile)], sems.at[k]))
        copies[-1].start()
    for copy in copies:
        copy.wait()


def diagonal_kernel(grid, factor_ref, inverse_ref, dbar_ref, rbar_ref, *refs):
    cores = grid.core[0]
    panel_refs, products, (out_ref, rbar_out_ref) = refs[:cores], refs[cores:-2], refs[-2:]
    me, my_col = lax.axis_index("row"), lax.axis_index("col")
    n, height, width = factor_ref.shape[0], grid.height, grid.width
    i, j = iotas((n, n))
    inverse = inverse_ref[...]
    si, sj = iotas((height, n))
    own_row = me * height + si
    weights = dot(hot(sj == own_row), inverse.T)
    inverse_perm = dot(inverse, hot(i == grid.relative_row(j, me)))
    product = unfold(add_pairs([ref[...] for ref in products]), n)
    proj = phi(dot(factor_ref[...].T, dbar_ref[...] - product))
    half = dot(weights, proj + proj.T)
    rows_sym, rows_perm = dot(half, inverse), dot(half, inverse_perm)
    high, low = split(rows_perm)
    panel_high, panel_low = split(jnp.concatenate([ref[...] for ref in panel_refs], axis=0))
    update = dot(high, panel_high, precision=None) + dot(low, panel_high, precision=None) + dot(high, panel_low, precision=None)
    rbar_out_ref[...] = rbar_ref[...] - update
    rows_kernel = jnp.where(sj < own_row, rows_sym, jnp.where(sj == own_row, 0.5 * rows_sym, 0.0))
    ci, cj = iotas((n, width))
    out_ref[...] = dot(rows_kernel, hot(ci == my_col * width + cj))


def call(kernel, out_shape, scratch=(), limit=8 * MIB, flops=0, specs=None):
    return pl.pallas_call(
        kernel,
        out_shape=out_shape,
        scratch_shapes=list(scratch),
        compiler_params=pltpu.CompilerParams(vmem_limit_bytes=limit),
        cost_estimate=pl.CostEstimate(flops=flops, bytes_accessed=1, transcendentals=0),
        **({"in_specs": specs} if specs else {}),
    )


def after(value, *others):
    return lax.optimization_barrier((value, *others))[0]


def add_pairs(terms):
    while len(terms) > 1:
        terms = [a + b for a, b in zip(terms[::2], terms[1::2])]
    return terms[0]


def make_body(rows, cols):
    def row_parts(value, step):
        count, stride = step
        return [value] + [swap(value, "row", rows, d * stride) for d in range(1, count)]

    def col_parts(value):
        return [value] + [swap(value, "col", cols, d) for d in range(1, cols)]

    def body(c_panel, cbar_in, factor, dbar_in, r_panel, rbar_in, b_block, bbar_in):
        n = factor.shape[0]
        depth, width = c_panel.shape
        height, breadth = r_panel.shape
        grid = Grid(rows, cols, height, width)

        cbar_parts, c_parts = col_parts(cbar_in.T), col_parts(c_panel.T)
        panel = jnp.concatenate(row_parts(r_panel, grid.z), axis=0)
        panel = jnp.concatenate(row_parts(panel, grid.x), axis=0)

        identity = call(identity_kernel, full((n, n)), flops=4 * 10 ** 9)()
        inverse, high, low = call(
            prepare_kernel,
            (full((n, n)), full((depth, breadth), BF16), full((depth, breadth), BF16)),
            [pltpu.VMEM((depth, breadth), F32), pltpu.SemaphoreType.DMA((8,))],
            limit=48 * MIB, flops=4000000000,
            specs=[pl.BlockSpec(memory_space=pltpu.VMEM)] * 2 + [pl.BlockSpec(memory_space=pltpu.HBM)],
        )(factor, identity, b_block)
        cbar_out_t, product, cbar_perm, stack = call(
            lambda *refs: cbar_kernel(grid, *refs),
            (full((width, depth)), full((8, (n // 16 + 1) * n)), full((n, depth)), full((2 * n, depth), BF16)),
            [pltpu.VMEM((n, depth), F32)] * 3, flops=1000000000,
        )(inverse, *cbar_parts, *c_parts)

        keep, send = call(trailing_kernel, (full((n // 2, breadth)),) * 2, flops=1000000000)(stack, high, low)
        summed = after(keep, panel) + swap(send, "row", rows, grid.core[1])
        product = add_pairs(row_parts(product, grid.core))
        product, summed = lax.optimization_barrier((product, summed))
        product = add_pairs(row_parts(product, grid.z_near))
        product, panel = lax.optimization_barrier((product, panel))
        panel_parts = row_parts(panel, grid.core)
        product = add_pairs(row_parts(product, grid.z_far))

        bbar_out = pl.pallas_call(
            bbar_kernel,
            in_specs=[pl.BlockSpec(memory_space=pltpu.VMEM)] * (2 + len(panel_parts)),
            out_specs=pl.BlockSpec(memory_space=pltpu.HBM),
            out_shape=full((depth, breadth)),
            scratch_shapes=[
                pltpu.VMEM((depth, breadth), F32), pltpu.VMEM((depth, 2 * n), BF16), pltpu.SemaphoreType.DMA((breadth // 256,))
            ],
            compiler_params=pltpu.CompilerParams(vmem_limit_bytes=16 * MIB),
            cost_estimate=pl.CostEstimate(flops=0, bytes_accessed=1, transcendentals=0),
        )(cbar_perm, bbar_in, *panel_parts)
        for count, stride in grid.order[1:]:
            own, *sends = summed.reshape(count, -1, breadth)
            summed = add_pairs([own] + [swap(value, "row", rows, d * stride) for d, value in enumerate(sends, 1)])
            if stride == grid.x[1]:
                product = after(product, summed)
        kernel_out, rbar = call(
            lambda *refs: diagonal_kernel(grid, *refs), (full((height, width)), full((height, breadth))), flops=0
        )(factor, inverse, dbar_in, rbar_in, *panel_parts, *row_parts(product, grid.x))
        return (cbar_out_t.T, bbar_out, kernel_out, rbar - summed)

    return body


def solution(mesh):
    spec = P("row", "col")
    in_specs = (spec, spec, P(), P(), spec, spec, spec, spec)
    return jax.shard_map(
        make_body(mesh.shape["row"], mesh.shape["col"]),
        mesh=mesh, in_specs=in_specs, out_specs=(spec,) * 4, check_vma=False,
    )
```

```python
import jax
import jax.numpy as jnp
from jax import lax
from jax.experimental import pallas as pl
from jax.experimental.pallas import tpu as pltpu
from jax.sharding import PartitionSpec as P

HIGHEST = lax.Precision.HIGHEST
HIGH = lax.Precision.HIGH
F32 = jnp.float32
BF16 = jnp.bfloat16
MIB = 1 << 20
LANES = 128


def dot(a, b, dims=((1,), (0,)), precision=HIGHEST):
    return lax.dot_general(a, b, (dims, ((), ())), precision=precision, preferred_element_type=F32)


def iotas(shape):
    return lax.broadcasted_iota(jnp.int32, shape, 0), lax.broadcasted_iota(jnp.int32, shape, 1)


def phi(matrix):
    i, j = iotas(matrix.shape)
    return jnp.where(i > j, matrix, jnp.where(i == j, 0.5 * matrix, 0.0))


def split(value):
    high = value.astype(BF16)
    return high, (value - high.astype(F32)).astype(BF16)


def split3(value):
    high = value.astype(BF16)
    rest = value - high.astype(F32)
    middle = rest.astype(BF16)
    return high, middle, (rest - middle.astype(F32)).astype(BF16)


def dot6(a, b):
    a1, a2, a3 = split3(a)
    b1, b2, b3 = split3(b)
    n = b.shape[1]
    left = jnp.concatenate([a1, a2], axis=1)
    right = jnp.concatenate([jnp.concatenate([b1, b1], axis=0), jnp.concatenate([b2, b2], axis=0)], axis=1)
    large = dot(left, right, precision=None)
    small = dot(jnp.concatenate([a1, a3], axis=1), jnp.concatenate([b3, b1], axis=0), precision=None)
    return large[:, :n] + (large[:, n:] + small)


def hot(cond):
    return jnp.where(cond, 1.0, 0.0).astype(F32)


def swap(value, axis, size, offset):
    return lax.ppermute(value, axis, [(i, i ^ offset) for i in range(size)])


def full(shape, dtype=F32):
    return jax.ShapeDtypeStruct(shape, dtype)


class Grid:
    def __init__(self, rows, cols, height, width):
        self.rows, self.cols, self.height, self.width = rows, cols, height, width
        cores, zs = 2, 4
        xs = rows // (cores * zs)
        self.core, self.x, self.z = (cores, 1), (xs, cores), (zs, xs * cores)
        self.z_near, self.z_far = (2, xs * cores), (2, 2 * xs * cores)
        self.order = (self.core, self.x, self.z)

    def offsets(self):
        found = [0]
        for count, stride in self.order:
            found = [base + d * stride for base in found for d in range(count)]
        return found

    def relative_row(self, position, me):
        block, inner = position // self.height, position % self.height
        offset = jnp.zeros_like(block)
        for count, stride in self.order[::-1]:
            offset = offset + (block % count) * stride
            block = block // count
        return (offset ^ me) * self.height + inner

    def permute_rows(self, ref, me):
        n, h = ref.shape[0], self.height
        if h % 8 == 0:
            return jnp.concatenate(
                [ref[pl.ds(pl.multiple_of((offset ^ me) * h, h), h), :] for offset in self.offsets()], axis=0
            )
        i, j = iotas((n, n))
        return dot(hot(j == self.relative_row(i, me)), ref[...])


def identity_kernel(out_ref):
    i, j = iotas(out_ref.shape)
    out_ref[...] = hot(i == j)


def prepare_kernel(factor_ref, identity_ref, b_hbm, inverse_t_ref, high_ref, low_ref, b_ref, sems):
    chunks = sems.shape[0]
    step = b_ref.shape[0] // chunks
    copies = [
        pltpu.make_async_copy(b_hbm.at[pl.ds(k * step, step)], b_ref.at[pl.ds(k * step, step)], sems.at[k])
        for k in range(chunks)
    ]
    for copy in copies:
        copy.start()

    def split_chunk(k):
        copies[k].wait()
        at = slice(k * step, (k + 1) * step)
        high_ref[at, :], low_ref[at, :] = split(b_ref[at, :])

    factor = factor_ref[...]
    n = factor.shape[0]
    i, j = iotas((n, n))
    diagonal = factor * identity_ref[...]
    recip_row = 1.0 / jnp.sum(diagonal, axis=0, keepdims=True)
    recip_col = 1.0 / jnp.sum(diagonal, axis=1, keepdims=True)
    size, level = 1, 0
    while size < n:
        below = (i // (2 * size) == j // (2 * size)) & ((i // size) % 2 == 1) & ((j // size) % 2 == 0)
        block = jnp.where(below, factor, 0.0)
        if level == 0:
            inverse = jnp.where(i == j, recip_row, -(recip_col * block * recip_row))
        else:
            inverse = inverse - dot6(dot6(inverse, block), inverse)
        if 2 <= level < 2 + chunks:
            split_chunk(level - 2)
        size, level = 2 * size, level + 1
    inverse_t_ref[...] = inverse.T
    for k in range(max(level - 2, 0), chunks):
        split_chunk(k)


def fold(matrix):
    n = matrix.shape[0]
    m = n // 2
    i, j = iotas((m, m))
    corner = matrix[m:, m:]
    mixed = jnp.where(i >= j, matrix[:m, :m], corner.T)
    diagonal = jnp.sum(jnp.where(i == j, corner, 0.0), axis=0, keepdims=True)
    top = jnp.concatenate([matrix[m:, :m], mixed], axis=1)
    last = jnp.broadcast_to(jnp.concatenate([diagonal, diagonal], axis=1), (8, n))
    return jnp.concatenate([top[k:k + 8] for k in range(0, m, 8)] + [last], axis=1)


def unfold(folded, n):
    folded = jnp.concatenate([folded[:, k:k + n] for k in range(0, folded.shape[1], n)], axis=0)
    m = n // 2
    i, j = iotas((m, m))
    mixed = folded[:m, m:]
    corner = jnp.where(i == j, folded[m:m + 1, :m], jnp.where(i > j, mixed.T, 0.0))
    upper = jnp.concatenate([jnp.where(i >= j, mixed, 0.0), jnp.zeros((m, m), F32)], axis=1)
    return jnp.concatenate([upper, jnp.concatenate([folded[:m, :m], corner], axis=1)], axis=0)


def cbar_kernel(grid, inverse_t_ref, *refs):
    cols = grid.cols
    cbar_refs, c_refs = refs[:cols], refs[cols:2 * cols]
    out_ref, product_ref, perm_ref, stack_ref, cbar, c, new = refs[2 * cols:]
    me, my_col = lax.axis_index("row"), lax.axis_index("col")
    n = inverse_t_ref.shape[0]
    for d in range(cols):
        at = pl.ds(pl.multiple_of((my_col ^ d) * grid.width, grid.width), grid.width)
        cbar[at, :] = cbar_refs[d][...]
        c[at, :] = c_refs[d][...]
    absolute = dot6(inverse_t_ref[...], cbar[...])
    new[...] = absolute
    perm = grid.permute_rows(new, me)
    perm_ref[...] = perm
    stack_ref[:n, :], stack_ref[n:, :] = split(perm)
    out_ref[...] = new[pl.ds(pl.multiple_of(my_col * grid.width, grid.width), grid.width), :]
    product_ref[...] = fold(dot(absolute, c[...], ((1,), (1,))))


def trailing_kernel(stack_ref, high_ref, low_ref, keep_ref, send_ref):
    n = stack_ref.shape[0] // 2
    breadth = high_ref.shape[1]
    tile = 256
    for k in range(breadth // tile):
        at = slice(k * tile, (k + 1) * tile)
        stacked = dot(stack_ref[...], high_ref[:, at], precision=None)
        total = stacked[:n] + stacked[n:] + dot(stack_ref[:n, :], low_ref[:, at], precision=None)
        keep_ref[:, at] = total[:n // 2]
        send_ref[:, at] = total[n // 2:]


def bbar_kernel(perm_ref, bbar_ref, *refs):
    panel_refs, (out_hbm, out_ref, left_ref, sems) = refs[:-4], refs[-4:]
    n = perm_ref.shape[0]
    left_ref[:, :n], left_ref[:, n:] = split(perm_ref[...].T)
    count = sems.shape[0]
    tile = bbar_ref.shape[1] // count
    copies = []
    for k in range(count):
        at = slice(k * tile, (k + 1) * tile)
        high, low = split(jnp.concatenate([ref[:, at] for ref in panel_refs], axis=0))
        update = dot(left_ref[...], jnp.concatenate([high, high], axis=0), precision=None)
        out_ref[:, at] = bbar_ref[:, at] - (update + dot(left_ref[:, :n], low, precision=None))
        copies.append(pltpu.make_async_copy(out_ref.at[:, pl.ds(k * tile, tile)], out_hbm.at[:, pl.ds(k * tile, tile)], sems.at[k]))
        copies[-1].start()
    for copy in copies:
        copy.wait()


def diagonal_kernel(grid, factor_ref, inverse_t_ref, dbar_ref, rbar_ref, *refs):
    cores = grid.core[0]
    panel_refs, products, (out_ref, rbar_out_ref) = refs[:cores], refs[cores:-2], refs[-2:]
    me, my_col = lax.axis_index("row"), lax.axis_index("col")
    n, height, width = factor_ref.shape[0], grid.height, grid.width
    product = unfold(add_pairs([ref[...] for ref in products]), n)
    proj = phi(dot6(factor_ref[...].T, dbar_ref[...] - product))
    if height % 8 == 0:
        weights = inverse_t_ref[pl.ds(pl.multiple_of(me * height, height), height), :]
    else:
        si, sj = iotas((height, n))
        weights = dot(hot(sj == me * height + si), inverse_t_ref[...])
    half = dot6(weights, proj + proj.T)
    both = jnp.concatenate([inverse_t_ref[...], grid.permute_rows(inverse_t_ref, me)], axis=0)
    rows = dot6(half, both.T)
    rows_sym = rows[:, :n]
    high, low = split(rows[:, n:])
    panel_high, panel_low = split(jnp.concatenate([ref[...] for ref in panel_refs], axis=0))
    update = dot(high, panel_high, precision=None) + dot(low, panel_high, precision=None) + dot(high, panel_low, precision=None)
    rbar_out_ref[...] = rbar_ref[...] - update
    si, sj = iotas((height, n))
    own_row = me * height + si
    rows_kernel = jnp.where(sj < own_row, rows_sym, jnp.where(sj == own_row, 0.5 * rows_sym, 0.0))
    out = rows_kernel[:, :width]
    for k in range(1, grid.cols):
        out = jnp.where(my_col == k, rows_kernel[:, k * width:(k + 1) * width], out)
    out_ref[...] = out


def call(kernel, out_shape, scratch=(), limit=8 * MIB, flops=0, specs=None):
    return pl.pallas_call(
        kernel,
        out_shape=out_shape,
        scratch_shapes=list(scratch),
        compiler_params=pltpu.CompilerParams(vmem_limit_bytes=limit),
        cost_estimate=pl.CostEstimate(flops=flops, bytes_accessed=1, transcendentals=0),
        **({"in_specs": specs} if specs else {}),
    )


def after(value, *others):
    return lax.optimization_barrier((value, *others))[0]


def add_pairs(terms):
    while len(terms) > 1:
        terms = [a + b for a, b in zip(terms[::2], terms[1::2])]
    return terms[0]


def make_body(rows, cols):
    def row_parts(value, step):
        count, stride = step
        return [value] + [swap(value, "row", rows, d * stride) for d in range(1, count)]

    def col_parts(value):
        return [value] + [swap(value, "col", cols, d) for d in range(1, cols)]

    def body(c_panel, cbar_in, factor, dbar_in, r_panel, rbar_in, b_block, bbar_in):
        n = factor.shape[0]
        depth, width = c_panel.shape
        height, breadth = r_panel.shape
        grid = Grid(rows, cols, height, width)

        cbar_parts, c_parts = col_parts(cbar_in.T), col_parts(c_panel.T)
        identity = call(identity_kernel, full((n, n)), flops=4 * 10 ** 9)()
        panel = jnp.concatenate(row_parts(r_panel, grid.z), axis=0)
        panel = jnp.concatenate(row_parts(panel, grid.x), axis=0)

        inverse_t, high, low = call(
            prepare_kernel,
            (full((n, n)), full((depth, breadth), BF16), full((depth, breadth), BF16)),
            [pltpu.VMEM((depth, breadth), F32), pltpu.SemaphoreType.DMA((8,))],
            limit=48 * MIB, flops=4000000000,
            specs=[pl.BlockSpec(memory_space=pltpu.VMEM)] * 2 + [pl.BlockSpec(memory_space=pltpu.HBM)],
        )(factor, identity, b_block)
        cbar_out_t, product, cbar_perm, stack = call(
            lambda *refs: cbar_kernel(grid, *refs),
            (full((width, depth)), full((8, (n // 16 + 1) * n)), full((n, depth)), full((2 * n, depth), BF16)),
            [pltpu.VMEM((n, depth), F32)] * 3, flops=1000000000,
        )(inverse_t, *cbar_parts, *c_parts)

        keep, send = call(trailing_kernel, (full((n // 2, breadth)),) * 2, flops=1000000000)(stack, high, low)
        summed = after(keep, panel) + swap(send, "row", rows, grid.core[1])
        product = add_pairs(row_parts(product, grid.core))
        product, summed = lax.optimization_barrier((product, summed))
        product = add_pairs(row_parts(product, grid.z_near))
        product, panel = lax.optimization_barrier((product, panel))
        panel_parts = row_parts(panel, grid.core)
        product = add_pairs(row_parts(product, grid.z_far))

        bbar_out = pl.pallas_call(
            bbar_kernel,
            in_specs=[pl.BlockSpec(memory_space=pltpu.VMEM)] * (2 + len(panel_parts)),
            out_specs=pl.BlockSpec(memory_space=pltpu.HBM),
            out_shape=full((depth, breadth)),
            scratch_shapes=[
                pltpu.VMEM((depth, breadth), F32), pltpu.VMEM((depth, 2 * n), BF16), pltpu.SemaphoreType.DMA((breadth // 256,))
            ],
            compiler_params=pltpu.CompilerParams(vmem_limit_bytes=16 * MIB),
            cost_estimate=pl.CostEstimate(flops=0, bytes_accessed=1, transcendentals=0),
        )(cbar_perm, bbar_in, *panel_parts)
        for count, stride in grid.order[1:]:
            own, *sends = summed.reshape(count, -1, breadth)
            summed = add_pairs([own] + [swap(value, "row", rows, d * stride) for d, value in enumerate(sends, 1)])
            if stride == grid.x[1]:
                product = after(product, summed)
        kernel_out, rbar = call(
            lambda *refs: diagonal_kernel(grid, *refs), (full((height, width)), full((height, breadth))), flops=0
        )(factor, inverse_t, dbar_in, rbar_in, *panel_parts, *row_parts(product, grid.x))
        return (cbar_out_t.T, bbar_out, kernel_out, rbar - summed)

    return body


def solution(mesh):
    spec = P("row", "col")
    in_specs = (spec, spec, P(), P(), spec, spec, spec, spec)
    return jax.shard_map(
        make_body(mesh.shape["row"], mesh.shape["col"]),
        mesh=mesh, in_specs=in_specs, out_specs=(spec,) * 4, check_vma=False,
    )
```

```python
import jax
import jax.numpy as jnp
from jax import lax
from jax.experimental import pallas as pl
from jax.experimental.pallas import tpu as pltpu
from jax.sharding import PartitionSpec as P

HIGHEST = lax.Precision.HIGHEST
HIGH = lax.Precision.HIGH
F32 = jnp.float32
BF16 = jnp.bfloat16
MIB = 1 << 20
LANES = 128


def dot(a, b, dims=((1,), (0,)), precision=HIGHEST):
    return lax.dot_general(a, b, (dims, ((), ())), precision=precision, preferred_element_type=F32)


def iotas(shape):
    return lax.broadcasted_iota(jnp.int32, shape, 0), lax.broadcasted_iota(jnp.int32, shape, 1)


def phi(matrix):
    i, j = iotas(matrix.shape)
    return jnp.where(i > j, matrix, jnp.where(i == j, 0.5 * matrix, 0.0))


def split(value):
    high = value.astype(BF16)
    return high, (value - high.astype(F32)).astype(BF16)


def split3(value):
    high = value.astype(BF16)
    rest = value - high.astype(F32)
    middle = rest.astype(BF16)
    return high, middle, (rest - middle.astype(F32)).astype(BF16)


def dot6(a, b):
    a1, a2, a3 = split3(a)
    b1, b2, b3 = split3(b)
    n = b.shape[1]
    left = jnp.concatenate([a1, a2], axis=1)
    right = jnp.concatenate([jnp.concatenate([b1, b1], axis=0), jnp.concatenate([b2, b2], axis=0)], axis=1)
    large = dot(left, right, precision=None)
    small = dot(jnp.concatenate([a1, a3], axis=1), jnp.concatenate([b3, b1], axis=0), precision=None)
    return large[:, :n] + (large[:, n:] + small)


def hot(cond):
    return jnp.where(cond, 1.0, 0.0).astype(F32)


def swap(value, axis, size, offset):
    return lax.ppermute(value, axis, [(i, i ^ offset) for i in range(size)])


def full(shape, dtype=F32):
    return jax.ShapeDtypeStruct(shape, dtype)


class Grid:
    def __init__(self, rows, cols, height, width):
        self.rows, self.cols, self.height, self.width = rows, cols, height, width
        cores, zs = 2, 4
        xs = rows // (cores * zs)
        self.core, self.x, self.z = (cores, 1), (xs, cores), (zs, xs * cores)
        self.z_near, self.z_far = (2, xs * cores), (2, 2 * xs * cores)
        self.order = (self.core, self.x, self.z)

    def offsets(self):
        found = [0]
        for count, stride in self.order:
            found = [base + d * stride for base in found for d in range(count)]
        return found

    def relative_row(self, position, me):
        block, inner = position // self.height, position % self.height
        offset = jnp.zeros_like(block)
        for count, stride in self.order[::-1]:
            offset = offset + (block % count) * stride
            block = block // count
        return (offset ^ me) * self.height + inner

    def permute_rows(self, ref, me):
        n, h = ref.shape[0], self.height
        if h % 8 == 0:
            return jnp.concatenate(
                [ref[pl.ds(pl.multiple_of((offset ^ me) * h, h), h), :] for offset in self.offsets()], axis=0
            )
        i, j = iotas((n, n))
        return dot(hot(j == self.relative_row(i, me)), ref[...])


def identity_kernel(out_ref):
    i, j = iotas(out_ref.shape)
    out_ref[...] = hot(i == j)


def prepare_kernel(factor_ref, identity_ref, b_hbm, inverse_t_ref, high_ref, low_ref, b_ref, sems):
    chunks = sems.shape[0]
    step = b_ref.shape[0] // chunks
    copies = [
        pltpu.make_async_copy(b_hbm.at[pl.ds(k * step, step)], b_ref.at[pl.ds(k * step, step)], sems.at[k])
        for k in range(chunks)
    ]
    for copy in copies:
        copy.start()

    def split_chunk(k):
        copies[k].wait()
        at = slice(k * step, (k + 1) * step)
        high_ref[at, :], low_ref[at, :] = split(b_ref[at, :])

    factor = factor_ref[...]
    n = factor.shape[0]
    i, j = iotas((n, n))
    diagonal = factor * identity_ref[...]
    recip_row = 1.0 / jnp.sum(diagonal, axis=0, keepdims=True)
    recip_col = 1.0 / jnp.sum(diagonal, axis=1, keepdims=True)
    size, level = 1, 0
    while size < n:
        below = (i // (2 * size) == j // (2 * size)) & ((i // size) % 2 == 1) & ((j // size) % 2 == 0)
        block = jnp.where(below, factor, 0.0)
        if level == 0:
            inverse = jnp.where(i == j, recip_row, -(recip_col * block * recip_row))
        else:
            inverse = inverse - dot6(dot6(inverse, block), inverse)
        if 2 <= level < 2 + chunks:
            split_chunk(level - 2)
        size, level = 2 * size, level + 1
    inverse_t_ref[...] = inverse.T
    for k in range(max(level - 2, 0), chunks):
        split_chunk(k)


def fold(matrix):
    n = matrix.shape[0]
    m = n // 2
    i, j = iotas((m, m))
    corner = matrix[m:, m:]
    mixed = jnp.where(i >= j, matrix[:m, :m], corner.T)
    diagonal = jnp.sum(jnp.where(i == j, corner, 0.0), axis=0, keepdims=True)
    top = jnp.concatenate([matrix[m:, :m], mixed], axis=1)
    last = jnp.broadcast_to(jnp.concatenate([diagonal, diagonal], axis=1), (8, n))
    return jnp.concatenate([top[k:k + 8] for k in range(0, m, 8)] + [last], axis=1)


def unfold(folded, n):
    folded = jnp.concatenate([folded[:, k:k + n] for k in range(0, folded.shape[1], n)], axis=0)
    m = n // 2
    i, j = iotas((m, m))
    mixed = folded[:m, m:]
    corner = jnp.where(i == j, folded[m:m + 1, :m], jnp.where(i > j, mixed.T, 0.0))
    upper = jnp.concatenate([jnp.where(i >= j, mixed, 0.0), jnp.zeros((m, m), F32)], axis=1)
    return jnp.concatenate([upper, jnp.concatenate([folded[:m, :m], corner], axis=1)], axis=0)


def place_parts(grid, refs, out_ref):
    for d, ref in enumerate(refs):
        start = (lax.axis_index("col") ^ d) * grid.width
        out_ref[pl.ds(pl.multiple_of(start, grid.width), grid.width), :] = ref[...]


def cbar_kernel(grid, inverse_t_ref, *refs):
    parts, (new_ref, out_ref, perm_ref, stack_ref, cbar) = refs[:grid.cols], refs[grid.cols:]
    me, my_col = lax.axis_index("row"), lax.axis_index("col")
    n = inverse_t_ref.shape[0]
    place_parts(grid, parts, cbar)
    new_ref[...] = dot6(inverse_t_ref[...], cbar[...])
    perm = grid.permute_rows(new_ref, me)
    perm_ref[...] = perm
    stack_ref[:n, :], stack_ref[n:, :] = split(perm)
    out_ref[...] = new_ref[pl.ds(pl.multiple_of(my_col * grid.width, grid.width), grid.width), :]


def product_kernel(grid, new_ref, *refs):
    parts, (product_ref, c) = refs[:grid.cols], refs[grid.cols:]
    place_parts(grid, parts, c)
    product_ref[...] = fold(dot(new_ref[...], c[...], ((1,), (1,))))


def trailing_kernel(stack_ref, high_ref, low_ref, keep_ref, send_ref):
    n = stack_ref.shape[0] // 2
    breadth = high_ref.shape[1]
    tile = 256
    for k in range(breadth // tile):
        at = slice(k * tile, (k + 1) * tile)
        stacked = dot(stack_ref[...], high_ref[:, at], precision=None)
        total = stacked[:n] + stacked[n:] + dot(stack_ref[:n, :], low_ref[:, at], precision=None)
        keep_ref[:, at] = total[:n // 2]
        send_ref[:, at] = total[n // 2:]


def bbar_kernel(perm_ref, bbar_ref, *refs):
    panel_refs, (out_hbm, out_ref, left_ref, sems) = refs[:-4], refs[-4:]
    n = perm_ref.shape[0]
    left_ref[:, :n], left_ref[:, n:] = split(perm_ref[...].T)
    count = sems.shape[0]
    tile = bbar_ref.shape[1] // count
    copies = []
    for k in range(count):
        at = slice(k * tile, (k + 1) * tile)
        high, low = split(jnp.concatenate([ref[:, at] for ref in panel_refs], axis=0))
        update = dot(left_ref[...], jnp.concatenate([high, high], axis=0), precision=None)
        out_ref[:, at] = bbar_ref[:, at] - (update + dot(left_ref[:, :n], low, precision=None))
        copies.append(pltpu.make_async_copy(out_ref.at[:, pl.ds(k * tile, tile)], out_hbm.at[:, pl.ds(k * tile, tile)], sems.at[k]))
        copies[-1].start()
    for copy in copies:
        copy.wait()


def diagonal_kernel(grid, factor_ref, inverse_t_ref, dbar_ref, rbar_ref, *refs):
    cores = grid.core[0]
    panel_refs, products, (out_ref, rbar_out_ref) = refs[:cores], refs[cores:-2], refs[-2:]
    me, my_col = lax.axis_index("row"), lax.axis_index("col")
    n, height, width = factor_ref.shape[0], grid.height, grid.width
    product = unfold(add_pairs([ref[...] for ref in products]), n)
    proj = phi(dot6(factor_ref[...].T, dbar_ref[...] - product))
    if height % 8 == 0:
        weights = inverse_t_ref[pl.ds(pl.multiple_of(me * height, height), height), :]
    else:
        si, sj = iotas((height, n))
        weights = dot(hot(sj == me * height + si), inverse_t_ref[...])
    half = dot6(weights, proj + proj.T)
    both = jnp.concatenate([inverse_t_ref[...], grid.permute_rows(inverse_t_ref, me)], axis=0)
    rows = dot6(half, both.T)
    rows_sym = rows[:, :n]
    high, low = split(rows[:, n:])
    panel_high, panel_low = split(jnp.concatenate([ref[...] for ref in panel_refs], axis=0))
    update = dot(high, panel_high, precision=None) + dot(low, panel_high, precision=None) + dot(high, panel_low, precision=None)
    rbar_out_ref[...] = rbar_ref[...] - update
    si, sj = iotas((height, n))
    own_row = me * height + si
    rows_kernel = jnp.where(sj < own_row, rows_sym, jnp.where(sj == own_row, 0.5 * rows_sym, 0.0))
    out = rows_kernel[:, :width]
    for k in range(1, grid.cols):
        out = jnp.where(my_col == k, rows_kernel[:, k * width:(k + 1) * width], out)
    out_ref[...] = out


def call(kernel, out_shape, scratch=(), limit=8 * MIB, flops=0, specs=None):
    return pl.pallas_call(
        kernel,
        out_shape=out_shape,
        scratch_shapes=list(scratch),
        compiler_params=pltpu.CompilerParams(vmem_limit_bytes=limit),
        cost_estimate=pl.CostEstimate(flops=flops, bytes_accessed=1, transcendentals=0),
        **({"in_specs": specs} if specs else {}),
    )


def after(value, *others):
    return lax.optimization_barrier((value, *others))[0]


def add_pairs(terms):
    while len(terms) > 1:
        terms = [a + b for a, b in zip(terms[::2], terms[1::2])]
    return terms[0]


def make_body(rows, cols):
    def row_parts(value, step):
        count, stride = step
        return [value] + [swap(value, "row", rows, d * stride) for d in range(1, count)]

    def col_parts(value):
        return [value] + [swap(value, "col", cols, d) for d in range(1, cols)]

    def body(c_panel, cbar_in, factor, dbar_in, r_panel, rbar_in, b_block, bbar_in):
        n = factor.shape[0]
        depth, width = c_panel.shape
        height, breadth = r_panel.shape
        grid = Grid(rows, cols, height, width)

        cbar_parts, c_parts = col_parts(cbar_in.T), col_parts(c_panel.T)
        identity = call(identity_kernel, full((n, n)), flops=4 * 10 ** 9)()
        panel = jnp.concatenate(row_parts(r_panel, grid.z), axis=0)
        panel = jnp.concatenate(row_parts(panel, grid.x), axis=0)

        inverse_t, high, low = call(
            prepare_kernel,
            (full((n, n)), full((depth, breadth), BF16), full((depth, breadth), BF16)),
            [pltpu.VMEM((depth, breadth), F32), pltpu.SemaphoreType.DMA((8,))],
            limit=48 * MIB, flops=4 * 10 ** 9,
            specs=[pl.BlockSpec(memory_space=pltpu.VMEM)] * 2 + [pl.BlockSpec(memory_space=pltpu.HBM)],
        )(factor, identity, b_block)
        cbar_new_t, cbar_out_t, cbar_perm, stack = call(
            lambda *refs: cbar_kernel(grid, *refs),
            (full((n, depth)), full((width, depth)), full((n, depth)), full((2 * n, depth), BF16)),
            [pltpu.VMEM((n, depth), F32)], flops=10 ** 9,
        )(inverse_t, *cbar_parts)
        keep, send = call(trailing_kernel, (full((n // 2, breadth)),) * 2, flops=10 ** 9)(stack, high, low)
        product = call(
            lambda *refs: product_kernel(grid, *refs), full((8, (n // 16 + 1) * n)), [pltpu.VMEM((n, depth), F32)],
        )(after(cbar_new_t, send), *c_parts)
        product = add_pairs(row_parts(product, grid.core))
        summed = after(keep, panel) + swap(send, "row", rows, grid.core[1])
        product, summed = lax.optimization_barrier((product, summed))
        panel = after(panel, summed)
        product_parts = row_parts(product, grid.z_near)
        panel_parts = row_parts(panel, grid.core)
        bbar_out = pl.pallas_call(
            bbar_kernel,
            in_specs=[pl.BlockSpec(memory_space=pltpu.VMEM)] * (2 + len(panel_parts)),
            out_specs=pl.BlockSpec(memory_space=pltpu.HBM),
            out_shape=full((depth, breadth)),
            scratch_shapes=[
                pltpu.VMEM((depth, breadth), F32), pltpu.VMEM((depth, 2 * n), BF16), pltpu.SemaphoreType.DMA((breadth // 256,))
            ],
            compiler_params=pltpu.CompilerParams(vmem_limit_bytes=16 * MIB),
            cost_estimate=pl.CostEstimate(flops=0, bytes_accessed=1, transcendentals=0),
        )(cbar_perm, bbar_in, *panel_parts)
        product = add_pairs(product_parts)
        product_parts = row_parts(product, grid.z_far)
        for count, stride in grid.order[1:]:
            own, *sends = summed.reshape(count, -1, breadth)
            got = [swap(value, "row", rows, d * stride) for d, value in enumerate(sends, 1)]
            summed = add_pairs([own] + got)
            if stride == grid.x[1]:
                product = add_pairs([after(product_parts[0], summed)] + product_parts[1:])
        kernel_out, rbar = call(
            lambda *refs: diagonal_kernel(grid, *refs), (full((height, width)), full((height, breadth))), flops=0
        )(factor, inverse_t, dbar_in, rbar_in, *panel_parts, *row_parts(product, grid.x))
        return (cbar_out_t.T, bbar_out, kernel_out, rbar - summed)

    return body


def solution(mesh):
    spec = P("row", "col")
    in_specs = (spec, spec, P(), P(), spec, spec, spec, spec)
    return jax.shard_map(
        make_body(mesh.shape["row"], mesh.shape["col"]),
        mesh=mesh, in_specs=in_specs, out_specs=(spec,) * 4, check_vma=False,
    )
```

```python
import jax
import jax.numpy as jnp
from jax import lax
from jax.experimental import pallas as pl
from jax.experimental.pallas import tpu as pltpu
from jax.sharding import PartitionSpec as P

HIGHEST = lax.Precision.HIGHEST
HIGH = lax.Precision.HIGH
F32 = jnp.float32
BF16 = jnp.bfloat16
MIB = 1 << 20
LANES = 128


def dot(a, b, dims=((1,), (0,)), precision=HIGHEST):
    return lax.dot_general(a, b, (dims, ((), ())), precision=precision, preferred_element_type=F32)


def iotas(shape):
    return lax.broadcasted_iota(jnp.int32, shape, 0), lax.broadcasted_iota(jnp.int32, shape, 1)


def phi(matrix):
    i, j = iotas(matrix.shape)
    return jnp.where(i > j, matrix, jnp.where(i == j, 0.5 * matrix, 0.0))


def split(value):
    high = value.astype(BF16)
    return high, (value - high.astype(F32)).astype(BF16)


def split3(value):
    high = value.astype(BF16)
    rest = value - high.astype(F32)
    middle = rest.astype(BF16)
    return high, middle, (rest - middle.astype(F32)).astype(BF16)


def dot6(a, b):
    a1, a2, a3 = split3(a)
    b1, b2, b3 = split3(b)
    n = b.shape[1]
    left = jnp.concatenate([a1, a2], axis=1)
    right = jnp.concatenate([jnp.concatenate([b1, b1], axis=0), jnp.concatenate([b2, b2], axis=0)], axis=1)
    large = dot(left, right, precision=None)
    small = dot(jnp.concatenate([a1, a3], axis=1), jnp.concatenate([b3, b1], axis=0), precision=None)
    return large[:, :n] + (large[:, n:] + small)


def hot(cond):
    return jnp.where(cond, 1.0, 0.0).astype(F32)


def swap(value, axis, size, offset):
    return lax.ppermute(value, axis, [(i, i ^ offset) for i in range(size)])


def full(shape, dtype=F32):
    return jax.ShapeDtypeStruct(shape, dtype)


class Grid:
    def __init__(self, rows, cols, height, width):
        self.rows, self.cols, self.height, self.width = rows, cols, height, width
        cores, zs = 2, 4
        xs = rows // (cores * zs)
        self.core, self.x, self.z = (cores, 1), (xs, cores), (zs, xs * cores)
        self.z_near, self.z_far = (2, xs * cores), (2, 2 * xs * cores)
        self.order = (self.core, self.x, self.z)

    def offsets(self):
        found = [0]
        for count, stride in self.order:
            found = [base + d * stride for base in found for d in range(count)]
        return found

    def relative_row(self, position, me):
        block, inner = position // self.height, position % self.height
        offset = jnp.zeros_like(block)
        for count, stride in self.order[::-1]:
            offset = offset + (block % count) * stride
            block = block // count
        return (offset ^ me) * self.height + inner

    def permute_rows(self, ref, me):
        n, h = ref.shape[0], self.height
        if h % 8 == 0:
            return jnp.concatenate(
                [ref[pl.ds(pl.multiple_of((offset ^ me) * h, h), h), :] for offset in self.offsets()], axis=0
            )
        i, j = iotas((n, n))
        return dot(hot(j == self.relative_row(i, me)), ref[...])


def identity_kernel(out_ref):
    i, j = iotas(out_ref.shape)
    out_ref[...] = hot(i == j)


def prepare_kernel(factor_ref, identity_ref, b_hbm, inverse_t_ref, high_ref, low_ref, b_ref, sems):
    chunks = sems.shape[0]
    step = b_ref.shape[0] // chunks
    copies = [
        pltpu.make_async_copy(b_hbm.at[pl.ds(k * step, step)], b_ref.at[pl.ds(k * step, step)], sems.at[k])
        for k in range(chunks)
    ]
    for copy in copies:
        copy.start()

    def split_chunk(k):
        copies[k].wait()
        at = slice(k * step, (k + 1) * step)
        high_ref[at, :], low_ref[at, :] = split(b_ref[at, :])

    factor = factor_ref[...]
    n = factor.shape[0]
    i, j = iotas((n, n))
    diagonal = factor * identity_ref[...]
    recip_row = 1.0 / jnp.sum(diagonal, axis=0, keepdims=True)
    recip_col = 1.0 / jnp.sum(diagonal, axis=1, keepdims=True)
    size, level = 1, 0
    while size < n:
        below = (i // (2 * size) == j // (2 * size)) & ((i // size) % 2 == 1) & ((j // size) % 2 == 0)
        block = jnp.where(below, factor, 0.0)
        if level == 0:
            inverse = jnp.where(i == j, recip_row, -(recip_col * block * recip_row))
        else:
            inverse = inverse - dot6(dot6(inverse, block), inverse)
        if 2 <= level < 2 + chunks:
            split_chunk(level - 2)
        size, level = 2 * size, level + 1
    inverse_t_ref[...] = inverse.T
    for k in range(max(level - 2, 0), chunks):
        split_chunk(k)


def fold(matrix):
    n = matrix.shape[0]
    m = n // 2
    i, j = iotas((m, m))
    corner = matrix[m:, m:]
    mixed = jnp.where(i >= j, matrix[:m, :m], corner.T)
    diagonal = jnp.sum(jnp.where(i == j, corner, 0.0), axis=0, keepdims=True)
    top = jnp.concatenate([matrix[m:, :m], mixed], axis=1)
    last = jnp.broadcast_to(jnp.concatenate([diagonal, diagonal], axis=1), (8, n))
    return jnp.concatenate([top[k:k + 8] for k in range(0, m, 8)] + [last], axis=1)


def unfold(folded, n):
    folded = jnp.concatenate([folded[:, k:k + n] for k in range(0, folded.shape[1], n)], axis=0)
    m = n // 2
    i, j = iotas((m, m))
    mixed = folded[:m, m:]
    corner = jnp.where(i == j, folded[m:m + 1, :m], jnp.where(i > j, mixed.T, 0.0))
    upper = jnp.concatenate([jnp.where(i >= j, mixed, 0.0), jnp.zeros((m, m), F32)], axis=1)
    return jnp.concatenate([upper, jnp.concatenate([folded[:m, :m], corner], axis=1)], axis=0)


def place_parts(grid, refs, out_ref):
    for d, ref in enumerate(refs):
        start = (lax.axis_index("col") ^ d) * grid.width
        out_ref[pl.ds(pl.multiple_of(start, grid.width), grid.width), :] = ref[...]


def cbar_kernel(grid, inverse_t_ref, *refs):
    parts, (new_ref, out_ref, perm_ref, stack_ref, cbar) = refs[:grid.cols], refs[grid.cols:]
    me, my_col = lax.axis_index("row"), lax.axis_index("col")
    n = inverse_t_ref.shape[0]
    place_parts(grid, parts, cbar)
    new_ref[...] = dot6(inverse_t_ref[...], cbar[...])
    perm = grid.permute_rows(new_ref, me)
    perm_ref[...] = perm
    stack_ref[:n, :], stack_ref[n:, :] = split(perm)
    out_ref[...] = new_ref[pl.ds(pl.multiple_of(my_col * grid.width, grid.width), grid.width), :]


def product_kernel(grid, new_ref, *refs):
    parts, (product_ref, c) = refs[:grid.cols], refs[grid.cols:]
    place_parts(grid, parts, c)
    product_ref[...] = fold(dot(new_ref[...], c[...], ((1,), (1,))))


def trailing_kernel(stack_ref, high_ref, low_ref, keep_ref, send_ref):
    n = stack_ref.shape[0] // 2
    breadth = high_ref.shape[1]
    tile = 256
    for k in range(breadth // tile):
        at = slice(k * tile, (k + 1) * tile)
        stacked = dot(stack_ref[...], high_ref[:, at], precision=None)
        total = stacked[:n] + stacked[n:] + dot(stack_ref[:n, :], low_ref[:, at], precision=None)
        keep_ref[:, at] = total[:n // 2]
        send_ref[:, at] = total[n // 2:]


def finish_kernel(grid, perm_ref, bbar_ref, factor_ref, inverse_t_ref, dbar_ref, rbar_ref, *refs):
    cores = grid.core[0]
    panel_refs, refs = refs[:cores], refs[cores:]
    products, (bbar_hbm, out_ref, rbar_out_ref, bbar_out, left_ref, sems) = refs[:-6], refs[-6:]
    me, my_col = lax.axis_index("row"), lax.axis_index("col")
    n, height, width = factor_ref.shape[0], grid.height, grid.width
    count = sems.shape[0]
    tile = bbar_ref.shape[1] // count
    left_ref[:, :n], left_ref[:, n:] = split(perm_ref[...].T)
    panels, copies = [], []

    def bbar_tile(k):
        at = slice(k * tile, (k + 1) * tile)
        high, low = split(jnp.concatenate([ref[:, at] for ref in panel_refs], axis=0))
        panels.append((high, low))
        update = dot(left_ref[...], jnp.concatenate([high, high], axis=0), precision=None)
        bbar_out[:, at] = bbar_ref[:, at] - (update + dot(left_ref[:, :n], low, precision=None))
        copies.append(pltpu.make_async_copy(bbar_out.at[:, pl.ds(k * tile, tile)], bbar_hbm.at[:, pl.ds(k * tile, tile)], sems.at[k]))
        copies[-1].start()

    product = unfold(add_pairs([ref[...] for ref in products]), n)
    bbar_tile(0)
    proj = phi(dot6(factor_ref[...].T, dbar_ref[...] - product))
    bbar_tile(1)
    if height % 8 == 0:
        weights = inverse_t_ref[pl.ds(pl.multiple_of(me * height, height), height), :]
    else:
        si, sj = iotas((height, n))
        weights = dot(hot(sj == me * height + si), inverse_t_ref[...])
    half = dot6(weights, proj + proj.T)
    bbar_tile(2)
    both = jnp.concatenate([inverse_t_ref[...], grid.permute_rows(inverse_t_ref, me)], axis=0)
    rows = dot6(half, both.T)
    for k in range(3, count):
        bbar_tile(k)
    rows_sym = rows[:, :n]
    high, low = split(rows[:, n:])
    for k, (panel_high, panel_low) in enumerate(panels):
        at = slice(k * tile, (k + 1) * tile)
        update = dot(high, panel_high, precision=None) + dot(low, panel_high, precision=None)
        rbar_out_ref[:, at] = rbar_ref[:, at] - (update + dot(high, panel_low, precision=None))
    si, sj = iotas((height, n))
    own_row = me * height + si
    rows_kernel = jnp.where(sj < own_row, rows_sym, jnp.where(sj == own_row, 0.5 * rows_sym, 0.0))
    out = rows_kernel[:, :width]
    for k in range(1, grid.cols):
        out = jnp.where(my_col == k, rows_kernel[:, k * width:(k + 1) * width], out)
    out_ref[...] = out
    for copy in copies:
        copy.wait()


def call(kernel, out_shape, scratch=(), limit=8 * MIB, flops=0, specs=None):
    return pl.pallas_call(
        kernel,
        out_shape=out_shape,
        scratch_shapes=list(scratch),
        compiler_params=pltpu.CompilerParams(vmem_limit_bytes=limit),
        cost_estimate=pl.CostEstimate(flops=flops, bytes_accessed=1, transcendentals=0),
        **({"in_specs": specs} if specs else {}),
    )


def after(value, *others):
    return lax.optimization_barrier((value, *others))[0]


def add_pairs(terms):
    while len(terms) > 1:
        terms = [a + b for a, b in zip(terms[::2], terms[1::2])]
    return terms[0]


def make_body(rows, cols):
    def row_parts(value, step):
        count, stride = step
        return [value] + [swap(value, "row", rows, d * stride) for d in range(count - 1, 0, -1)][::-1]

    def col_parts(value):
        return [value] + [swap(value, "col", cols, d) for d in range(1, cols)]

    def body(c_panel, cbar_in, factor, dbar_in, r_panel, rbar_in, b_block, bbar_in):
        n = factor.shape[0]
        depth, width = c_panel.shape
        height, breadth = r_panel.shape
        grid = Grid(rows, cols, height, width)

        cbar_parts, c_parts = col_parts(cbar_in.T), col_parts(c_panel.T)
        identity = call(identity_kernel, full((n, n)), flops=4 * 10 ** 9)()
        panel = jnp.concatenate(row_parts(r_panel, grid.z), axis=0)
        panel = jnp.concatenate(row_parts(panel, grid.x), axis=0)

        inverse_t, high, low = call(
            prepare_kernel,
            (full((n, n)), full((depth, breadth), BF16), full((depth, breadth), BF16)),
            [pltpu.VMEM((depth, breadth), F32), pltpu.SemaphoreType.DMA((8,))],
            limit=48 * MIB, flops=4 * 10 ** 9,
            specs=[pl.BlockSpec(memory_space=pltpu.VMEM)] * 2 + [pl.BlockSpec(memory_space=pltpu.HBM)],
        )(factor, identity, b_block)
        cbar_new_t, cbar_out_t, cbar_perm, stack = call(
            lambda *refs: cbar_kernel(grid, *refs),
            (full((n, depth)), full((width, depth)), full((n, depth)), full((2 * n, depth), BF16)),
            [pltpu.VMEM((n, depth), F32)], flops=10 ** 9,
        )(inverse_t, *cbar_parts)
        keep, send = call(trailing_kernel, (full((n // 2, breadth)),) * 2, flops=10 ** 9)(stack, high, low)
        product = call(
            lambda *refs: product_kernel(grid, *refs), full((8, (n // 16 + 1) * n)), [pltpu.VMEM((n, depth), F32)],
        )(after(cbar_new_t, send), *c_parts)
        product = add_pairs(row_parts(product, grid.core))
        summed = keep + swap(send, "row", rows, grid.core[1])
        product, summed = lax.optimization_barrier((product, summed))
        panel = after(panel, summed)
        product = add_pairs(row_parts(product, grid.z_near))
        product_parts = row_parts(product, grid.z_far)
        panel_parts = row_parts(panel, grid.core)
        product = add_pairs(product_parts)
        for count, stride in grid.order[1:]:
            own, *sends = summed.reshape(count, -1, breadth)
            got = [swap(value, "row", rows, d * stride) for d, value in list(enumerate(sends, 1))[::-1]][::-1]
            if stride == grid.x[1]:
                own = after(own, product)
            summed = add_pairs([own] + got[::-1])
            if stride == grid.x[1]:
                dbar_in = after(dbar_in, summed)
        vmem = pl.BlockSpec(memory_space=pltpu.VMEM)
        product_parts = row_parts(product, grid.x)
        bbar_out, kernel_out, rbar = pl.pallas_call(
            lambda *refs: finish_kernel(grid, *refs),
            in_specs=[vmem] * (6 + len(panel_parts) + len(product_parts)),
            out_specs=[pl.BlockSpec(memory_space=pltpu.HBM), vmem, vmem],
            out_shape=(full((depth, breadth)), full((height, width)), full((height, breadth))),
            scratch_shapes=[
                pltpu.VMEM((depth, breadth), F32), pltpu.VMEM((depth, 2 * n), BF16), pltpu.SemaphoreType.DMA((breadth // 256,))
            ],
            compiler_params=pltpu.CompilerParams(vmem_limit_bytes=16 * MIB),
            cost_estimate=pl.CostEstimate(flops=10 ** 9, bytes_accessed=1, transcendentals=0),
        )(cbar_perm, bbar_in, factor, inverse_t, dbar_in, rbar_in, *panel_parts, *product_parts)
        return (cbar_out_t.T, bbar_out, kernel_out, rbar - summed)

    return body


def solution(mesh):
    spec = P("row", "col")
    in_specs = (spec, spec, P(), P(), spec, spec, spec, spec)
    return jax.shard_map(
        make_body(mesh.shape["row"], mesh.shape["col"]),
        mesh=mesh, in_specs=in_specs, out_specs=(spec,) * 4, check_vma=False,
    )
```

```python
import jax
import jax.numpy as jnp
from jax import lax
from jax.experimental import pallas as pl
from jax.experimental.pallas import tpu as pltpu
from jax.sharding import PartitionSpec as P

HIGHEST = lax.Precision.HIGHEST
HIGH = lax.Precision.HIGH
F32 = jnp.float32
BF16 = jnp.bfloat16
MIB = 1 << 20
LANES = 128


def dot(a, b, dims=((1,), (0,)), precision=HIGHEST):
    return lax.dot_general(a, b, (dims, ((), ())), precision=precision, preferred_element_type=F32)


def iotas(shape):
    return lax.broadcasted_iota(jnp.int32, shape, 0), lax.broadcasted_iota(jnp.int32, shape, 1)


def phi(matrix):
    i, j = iotas(matrix.shape)
    return jnp.where(i > j, matrix, jnp.where(i == j, 0.5 * matrix, 0.0))


def split(value):
    high = value.astype(BF16)
    return high, (value - high.astype(F32)).astype(BF16)


def split3(value):
    high = value.astype(BF16)
    rest = value - high.astype(F32)
    middle = rest.astype(BF16)
    return high, middle, (rest - middle.astype(F32)).astype(BF16)


def dot6(a, b):
    a1, a2, a3 = split3(a)
    b1, b2, b3 = split3(b)
    n = b.shape[1]
    left = jnp.concatenate([a1, a2], axis=1)
    right = jnp.concatenate([jnp.concatenate([b1, b1], axis=0), jnp.concatenate([b2, b2], axis=0)], axis=1)
    large = dot(left, right, precision=None)
    small = dot(jnp.concatenate([a1, a3], axis=1), jnp.concatenate([b3, b1], axis=0), precision=None)
    return large[:, :n] + (large[:, n:] + small)


def hot(cond):
    return jnp.where(cond, 1.0, 0.0).astype(F32)


def swap(value, axis, size, offset):
    return lax.ppermute(value, axis, [(i, i ^ offset) for i in range(size)])


def full(shape, dtype=F32):
    return jax.ShapeDtypeStruct(shape, dtype)


class Grid:
    def __init__(self, rows, cols, height, width):
        self.rows, self.cols, self.height, self.width = rows, cols, height, width
        cores, zs = 2, 4
        xs = rows // (cores * zs)
        self.core, self.x, self.z = (cores, 1), (xs, cores), (zs, xs * cores)
        self.z_near, self.z_far = (2, xs * cores), (2, 2 * xs * cores)
        self.order = (self.core, self.x, self.z)

    def offsets(self):
        found = [0]
        for count, stride in self.order:
            found = [base + d * stride for base in found for d in range(count)]
        return found

    def relative_row(self, position, me):
        block, inner = position // self.height, position % self.height
        offset = jnp.zeros_like(block)
        for count, stride in self.order[::-1]:
            offset = offset + (block % count) * stride
            block = block // count
        return (offset ^ me) * self.height + inner

    def permute_rows(self, ref, me):
        n, h = ref.shape[0], self.height
        if h % 8 == 0:
            return jnp.concatenate(
                [ref[pl.ds(pl.multiple_of((offset ^ me) * h, h), h), :] for offset in self.offsets()], axis=0
            )
        i, j = iotas((n, n))
        return dot(hot(j == self.relative_row(i, me)), ref[...])


def identity_kernel(out_ref):
    i, j = iotas(out_ref.shape)
    out_ref[...] = hot(i == j)


def prepare_kernel(factor_ref, identity_ref, b_hbm, inverse_t_ref, high_ref, low_ref, b_ref, sems):
    chunks = sems.shape[0]
    step = b_ref.shape[0] // chunks
    copies = [
        pltpu.make_async_copy(b_hbm.at[pl.ds(k * step, step)], b_ref.at[pl.ds(k * step, step)], sems.at[k])
        for k in range(chunks)
    ]
    for copy in copies:
        copy.start()

    def split_chunk(k):
        copies[k].wait()
        at = slice(k * step, (k + 1) * step)
        high_ref[at, :], low_ref[at, :] = split(b_ref[at, :])

    factor = factor_ref[...]
    n = factor.shape[0]
    i, j = iotas((n, n))
    diagonal = factor * identity_ref[...]
    recip_row = 1.0 / jnp.sum(diagonal, axis=0, keepdims=True)
    recip_col = 1.0 / jnp.sum(diagonal, axis=1, keepdims=True)
    size, level = 1, 0
    while size < n:
        below = (i // (2 * size) == j // (2 * size)) & ((i // size) % 2 == 1) & ((j // size) % 2 == 0)
        block = jnp.where(below, factor, 0.0)
        if level == 0:
            inverse = jnp.where(i == j, recip_row, -(recip_col * block * recip_row))
        else:
            inverse = inverse - dot6(dot6(inverse, block), inverse)
        if 2 <= level < 2 + chunks:
            split_chunk(level - 2)
        size, level = 2 * size, level + 1
    inverse_t_ref[...] = inverse.T
    for k in range(max(level - 2, 0), chunks):
        split_chunk(k)


def fold(matrix):
    n = matrix.shape[0]
    m = n // 2
    i, j = iotas((m, m))
    corner = matrix[m:, m:]
    mixed = jnp.where(i >= j, matrix[:m, :m], corner.T)
    diagonal = jnp.sum(jnp.where(i == j, corner, 0.0), axis=0, keepdims=True)
    top = jnp.concatenate([matrix[m:, :m], mixed], axis=1)
    last = jnp.broadcast_to(jnp.concatenate([diagonal, diagonal], axis=1), (8, n))
    return jnp.concatenate([top[k:k + 8] for k in range(0, m, 8)] + [last], axis=1)


def unfold(folded, n):
    folded = jnp.concatenate([folded[:, k:k + n] for k in range(0, folded.shape[1], n)], axis=0)
    m = n // 2
    i, j = iotas((m, m))
    mixed = folded[:m, m:]
    corner = jnp.where(i == j, folded[m:m + 1, :m], jnp.where(i > j, mixed.T, 0.0))
    upper = jnp.concatenate([jnp.where(i >= j, mixed, 0.0), jnp.zeros((m, m), F32)], axis=1)
    return jnp.concatenate([upper, jnp.concatenate([folded[:m, :m], corner], axis=1)], axis=0)


def place_parts(grid, refs, out_ref):
    for d, ref in enumerate(refs):
        start = (lax.axis_index("col") ^ d) * grid.width
        out_ref[pl.ds(pl.multiple_of(start, grid.width), grid.width), :] = ref[...]


def cbar_kernel(grid, inverse_t_ref, *refs):
    parts, (new_ref, out_ref, perm_ref, stack_ref, cbar) = refs[:grid.cols], refs[grid.cols:]
    me, my_col = lax.axis_index("row"), lax.axis_index("col")
    n = inverse_t_ref.shape[0]
    place_parts(grid, parts, cbar)
    new_ref[...] = dot6(inverse_t_ref[...], cbar[...])
    perm = grid.permute_rows(new_ref, me)
    perm_ref[...] = perm
    stack_ref[:n, :], stack_ref[n:, :] = split(perm)
    out_ref[...] = new_ref[pl.ds(pl.multiple_of(my_col * grid.width, grid.width), grid.width), :]


def product_kernel(grid, new_ref, *refs):
    parts, (product_ref, c) = refs[:grid.cols], refs[grid.cols:]
    place_parts(grid, parts, c)
    product_ref[...] = fold(dot(new_ref[...], c[...], ((1,), (1,))))


def trailing_kernel(stack_ref, high_ref, low_ref, keep_ref, send_ref):
    n = stack_ref.shape[0] // 2
    breadth = high_ref.shape[1]
    tile = 256
    for k in range(breadth // tile):
        at = slice(k * tile, (k + 1) * tile)
        stacked = dot(stack_ref[...], high_ref[:, at], precision=None)
        total = stacked[:n] + stacked[n:] + dot(stack_ref[:n, :], low_ref[:, at], precision=None)
        keep_ref[:, at] = total[:n // 2]
        send_ref[:, at] = total[n // 2:]


def finish_kernel(grid, perm_ref, bbar_ref, factor_ref, inverse_t_ref, dbar_ref, rbar_ref, *refs):
    cores = grid.core[0]
    panel_refs, refs = refs[:cores], refs[cores:]
    products, (bbar_hbm, out_ref, rbar_out_ref, bbar_out, left_ref, sems) = refs[:-6], refs[-6:]
    me, my_col = lax.axis_index("row"), lax.axis_index("col")
    n, height, width = factor_ref.shape[0], grid.height, grid.width
    count = sems.shape[0]
    tile = bbar_ref.shape[1] // count
    left_ref[:, :n], left_ref[:, n:] = split(perm_ref[...].T)
    panels, copies = [], []

    def bbar_tile(k):
        at = slice(k * tile, (k + 1) * tile)
        high, low = split(jnp.concatenate([ref[:, at] for ref in panel_refs], axis=0))
        panels.append((high, low))
        update = dot(left_ref[...], jnp.concatenate([high, high], axis=0), precision=None)
        bbar_out[:, at] = bbar_ref[:, at] - (update + dot(left_ref[:, :n], low, precision=None))
        copies.append(pltpu.make_async_copy(bbar_out.at[:, pl.ds(k * tile, tile)], bbar_hbm.at[:, pl.ds(k * tile, tile)], sems.at[k]))
        copies[-1].start()

    product = unfold(add_pairs([ref[...] for ref in products]), n)
    bbar_tile(0)
    proj = phi(dot6(factor_ref[...].T, dbar_ref[...] - product))
    bbar_tile(1)
    if height % 8 == 0:
        weights = inverse_t_ref[pl.ds(pl.multiple_of(me * height, height), height), :]
    else:
        si, sj = iotas((height, n))
        weights = dot(hot(sj == me * height + si), inverse_t_ref[...])
    half = dot6(weights, proj + proj.T)
    bbar_tile(2)
    both = jnp.concatenate([inverse_t_ref[...], grid.permute_rows(inverse_t_ref, me)], axis=0)
    rows = dot6(half, both.T)
    for k in range(3, count):
        bbar_tile(k)
    rows_sym = rows[:, :n]
    high, low = split(rows[:, n:])
    for k, (panel_high, panel_low) in enumerate(panels):
        at = slice(k * tile, (k + 1) * tile)
        update = dot(high, panel_high, precision=None) + dot(low, panel_high, precision=None)
        rbar_out_ref[:, at] = rbar_ref[:, at] - (update + dot(high, panel_low, precision=None))
    si, sj = iotas((height, n))
    own_row = me * height + si
    rows_kernel = jnp.where(sj < own_row, rows_sym, jnp.where(sj == own_row, 0.5 * rows_sym, 0.0))
    out = rows_kernel[:, :width]
    for k in range(1, grid.cols):
        out = jnp.where(my_col == k, rows_kernel[:, k * width:(k + 1) * width], out)
    out_ref[...] = out
    for copy in copies:
        copy.wait()


def call(kernel, out_shape, scratch=(), limit=8 * MIB, flops=0, specs=None):
    return pl.pallas_call(
        kernel,
        out_shape=out_shape,
        scratch_shapes=list(scratch),
        compiler_params=pltpu.CompilerParams(vmem_limit_bytes=limit),
        cost_estimate=pl.CostEstimate(flops=flops, bytes_accessed=1, transcendentals=0),
        **({"in_specs": specs} if specs else {}),
    )


def after(value, *others):
    return lax.optimization_barrier((value, *others))[0]


def add_pairs(terms):
    while len(terms) > 1:
        terms = [a + b for a, b in zip(terms[::2], terms[1::2])]
    return terms[0]


def make_body(rows, cols):
    def row_parts(value, step):
        count, stride = step
        return [value] + [swap(value, "row", rows, d * stride) for d in range(count - 1, 0, -1)][::-1]

    def col_parts(value):
        return [value] + [swap(value, "col", cols, d) for d in range(1, cols)]

    def body(c_panel, cbar_in, factor, dbar_in, r_panel, rbar_in, b_block, bbar_in):
        n = factor.shape[0]
        depth, width = c_panel.shape
        height, breadth = r_panel.shape
        grid = Grid(rows, cols, height, width)

        cbar_parts, c_parts = col_parts(cbar_in.T), col_parts(c_panel.T)
        identity = call(identity_kernel, full((n, n)), flops=4 * 10 ** 9)()
        panel = jnp.concatenate(row_parts(r_panel, grid.z), axis=0)
        panel = jnp.concatenate(row_parts(panel, grid.x), axis=0)

        inverse_t, high, low = call(
            prepare_kernel,
            (full((n, n)), full((depth, breadth), BF16), full((depth, breadth), BF16)),
            [pltpu.VMEM((depth, breadth), F32), pltpu.SemaphoreType.DMA((8,))],
            limit=48 * MIB, flops=4 * 10 ** 9,
            specs=[pl.BlockSpec(memory_space=pltpu.VMEM)] * 2 + [pl.BlockSpec(memory_space=pltpu.HBM)],
        )(factor, identity, b_block)
        cbar_new_t, cbar_out_t, cbar_perm, stack = call(
            lambda *refs: cbar_kernel(grid, *refs),
            (full((n, depth)), full((width, depth)), full((n, depth)), full((2 * n, depth), BF16)),
            [pltpu.VMEM((n, depth), F32)], flops=10 ** 9,
        )(inverse_t, *cbar_parts)
        keep, send = call(trailing_kernel, (full((n // 2, breadth)),) * 2, flops=10 ** 9)(stack, high, low)
        product = call(
            lambda *refs: product_kernel(grid, *refs), full((8, (n // 16 + 1) * n)), [pltpu.VMEM((n, depth), F32)],
        )(after(cbar_new_t, send), *c_parts)
        product = add_pairs(row_parts(product, grid.core))
        summed = keep + swap(send, "row", rows, grid.core[1])
        product, summed = lax.optimization_barrier((product, summed))
        product = add_pairs(row_parts(product, grid.z_near))
        product_parts = row_parts(product, grid.z_far)
        product = add_pairs(product_parts)
        for count, stride in grid.order[1:]:
            own, *sends = summed.reshape(count, -1, breadth)
            got = [swap(value, "row", rows, d * stride) for d, value in list(enumerate(sends, 1))[::-1]][::-1]
            if stride == grid.x[1]:
                own = after(own, product)
                panel = after(panel, product)
            summed = add_pairs([own] + got[::-1])
            if stride == grid.x[1]:
                dbar_in = after(dbar_in, summed)
        panel_parts = row_parts(panel, grid.core)
        vmem = pl.BlockSpec(memory_space=pltpu.VMEM)
        product_parts = row_parts(product, grid.x)
        bbar_out, kernel_out, rbar = pl.pallas_call(
            lambda *refs: finish_kernel(grid, *refs),
            in_specs=[vmem] * (6 + len(panel_parts) + len(product_parts)),
            out_specs=[pl.BlockSpec(memory_space=pltpu.HBM), vmem, vmem],
            out_shape=(full((depth, breadth)), full((height, width)), full((height, breadth))),
            scratch_shapes=[
                pltpu.VMEM((depth, breadth), F32), pltpu.VMEM((depth, 2 * n), BF16), pltpu.SemaphoreType.DMA((breadth // 256,))
            ],
            compiler_params=pltpu.CompilerParams(vmem_limit_bytes=16 * MIB),
            cost_estimate=pl.CostEstimate(flops=10 ** 9, bytes_accessed=1, transcendentals=0),
        )(cbar_perm, bbar_in, factor, inverse_t, dbar_in, rbar_in, *panel_parts, *product_parts)
        return (cbar_out_t.T, bbar_out, kernel_out, rbar - summed)

    return body


def solution(mesh):
    spec = P("row", "col")
    in_specs = (spec, spec, P(), P(), spec, spec, spec, spec)
    return jax.shard_map(
        make_body(mesh.shape["row"], mesh.shape["col"]),
        mesh=mesh, in_specs=in_specs, out_specs=(spec,) * 4, check_vma=False,
    )
```

```python
import jax
import jax.numpy as jnp
from jax import lax
from jax.experimental import pallas as pl
from jax.experimental.pallas import tpu as pltpu
from jax.sharding import PartitionSpec as P

HIGHEST = lax.Precision.HIGHEST
HIGH = lax.Precision.HIGH
F32 = jnp.float32
BF16 = jnp.bfloat16
MIB = 1 << 20
LANES = 128


def dot(a, b, dims=((1,), (0,)), precision=HIGHEST):
    return lax.dot_general(a, b, (dims, ((), ())), precision=precision, preferred_element_type=F32)


def iotas(shape):
    return lax.broadcasted_iota(jnp.int32, shape, 0), lax.broadcasted_iota(jnp.int32, shape, 1)


def phi(matrix):
    i, j = iotas(matrix.shape)
    return jnp.where(i > j, matrix, jnp.where(i == j, 0.5 * matrix, 0.0))


def split(value):
    high = value.astype(BF16)
    return high, (value - high.astype(F32)).astype(BF16)


def split3(value):
    high = value.astype(BF16)
    rest = value - high.astype(F32)
    middle = rest.astype(BF16)
    return high, middle, (rest - middle.astype(F32)).astype(BF16)


def dot6(a, b):
    a1, a2, a3 = split3(a)
    b1, b2, b3 = split3(b)
    n = b.shape[1]
    left = jnp.concatenate([a1, a2], axis=1)
    right = jnp.concatenate([jnp.concatenate([b1, b1], axis=0), jnp.concatenate([b2, b2], axis=0)], axis=1)
    large = dot(left, right, precision=None)
    small = dot(jnp.concatenate([a1, a3], axis=1), jnp.concatenate([b3, b1], axis=0), precision=None)
    return large[:, :n] + (large[:, n:] + small)


def hot(cond):
    return jnp.where(cond, 1.0, 0.0).astype(F32)


def swap(value, axis, size, offset):
    return lax.ppermute(value, axis, [(i, i ^ offset) for i in range(size)])


def full(shape, dtype=F32):
    return jax.ShapeDtypeStruct(shape, dtype)


class Grid:
    def __init__(self, rows, cols, height, width):
        self.rows, self.cols, self.height, self.width = rows, cols, height, width
        cores, zs = 2, 4
        xs = rows // (cores * zs)
        self.core, self.x, self.z = (cores, 1), (xs, cores), (zs, xs * cores)
        self.z_near, self.z_far = (2, xs * cores), (2, 2 * xs * cores)
        self.order = (self.core, self.x, self.z)

    def offsets(self):
        found = [0]
        for count, stride in self.order:
            found = [base + d * stride for base in found for d in range(count)]
        return found

    def relative_row(self, position, me):
        block, inner = position // self.height, position % self.height
        offset = jnp.zeros_like(block)
        for count, stride in self.order[::-1]:
            offset = offset + (block % count) * stride
            block = block // count
        return (offset ^ me) * self.height + inner

    def permute_rows(self, ref, me):
        n, h = ref.shape[0], self.height
        if h % 8 == 0:
            return jnp.concatenate(
                [ref[pl.ds(pl.multiple_of((offset ^ me) * h, h), h), :] for offset in self.offsets()], axis=0
            )
        i, j = iotas((n, n))
        return dot(hot(j == self.relative_row(i, me)), ref[...])


def identity_kernel(out_ref):
    i, j = iotas(out_ref.shape)
    out_ref[...] = hot(i == j)


def prepare_kernel(factor_ref, identity_ref, b_hbm, inverse_t_ref, high_ref, low_ref, b_ref, sems):
    chunks = sems.shape[0]
    step = b_ref.shape[0] // chunks
    copies = [
        pltpu.make_async_copy(b_hbm.at[pl.ds(k * step, step)], b_ref.at[pl.ds(k * step, step)], sems.at[k])
        for k in range(chunks)
    ]
    for copy in copies:
        copy.start()

    def split_chunk(k):
        copies[k].wait()
        at = slice(k * step, (k + 1) * step)
        high_ref[at, :], low_ref[at, :] = split(b_ref[at, :])

    factor = factor_ref[...]
    n = factor.shape[0]
    i, j = iotas((n, n))
    diagonal = factor * identity_ref[...]
    recip_row = 1.0 / jnp.sum(diagonal, axis=0, keepdims=True)
    recip_col = 1.0 / jnp.sum(diagonal, axis=1, keepdims=True)
    size, done = 16, 0
    nilpotent = jnp.where((i // size == j // size) & (i > j), -(recip_col * factor), 0.0)
    second = dot6(nilpotent, nilpotent)
    fourth = dot6(second, second)
    series = identity_ref[...] + nilpotent + second + dot6(nilpotent, second)
    eighth = dot6(fourth, fourth)
    series = series + dot6(series, fourth)
    inverse = (series + dot6(series, eighth)) * recip_row
    while size < n:
        below = (i // (2 * size) == j // (2 * size)) & ((i // size) % 2 == 1) & ((j // size) % 2 == 0)
        block = jnp.where(below, factor, 0.0)
        inverse = inverse - dot6(dot6(inverse, block), inverse)
        if done < chunks:
            split_chunk(done)
            done += 1
        size *= 2
    inverse_t_ref[...] = inverse.T
    for k in range(done, chunks):
        split_chunk(k)


def fold(matrix):
    n = matrix.shape[0]
    m = n // 2
    i, j = iotas((m, m))
    corner = matrix[m:, m:]
    mixed = jnp.where(i >= j, matrix[:m, :m], corner.T)
    diagonal = jnp.sum(jnp.where(i == j, corner, 0.0), axis=0, keepdims=True)
    top = jnp.concatenate([matrix[m:, :m], mixed], axis=1)
    last = jnp.broadcast_to(jnp.concatenate([diagonal, diagonal], axis=1), (8, n))
    return jnp.concatenate([top[k:k + 8] for k in range(0, m, 8)] + [last], axis=1)


def unfold(folded, n):
    folded = jnp.concatenate([folded[:, k:k + n] for k in range(0, folded.shape[1], n)], axis=0)
    m = n // 2
    i, j = iotas((m, m))
    mixed = folded[:m, m:]
    corner = jnp.where(i == j, folded[m:m + 1, :m], jnp.where(i > j, mixed.T, 0.0))
    upper = jnp.concatenate([jnp.where(i >= j, mixed, 0.0), jnp.zeros((m, m), F32)], axis=1)
    return jnp.concatenate([upper, jnp.concatenate([folded[:m, :m], corner], axis=1)], axis=0)


def place_parts(grid, refs, out_ref):
    for d, ref in enumerate(refs):
        start = (lax.axis_index("col") ^ d) * grid.width
        out_ref[pl.ds(pl.multiple_of(start, grid.width), grid.width), :] = ref[...]


def cbar_kernel(grid, inverse_t_ref, *refs):
    parts, (new_ref, out_ref, perm_ref, stack_ref, cbar) = refs[:grid.cols], refs[grid.cols:]
    me, my_col = lax.axis_index("row"), lax.axis_index("col")
    n = inverse_t_ref.shape[0]
    place_parts(grid, parts, cbar)
    new_ref[...] = dot6(inverse_t_ref[...], cbar[...])
    perm = grid.permute_rows(new_ref, me)
    perm_ref[...] = perm
    stack_ref[:n, :], stack_ref[n:, :] = split(perm)
    out_ref[...] = new_ref[pl.ds(pl.multiple_of(my_col * grid.width, grid.width), grid.width), :]


def product_kernel(grid, new_ref, *refs):
    parts, (product_ref, c) = refs[:grid.cols], refs[grid.cols:]
    place_parts(grid, parts, c)
    product_ref[...] = fold(dot(new_ref[...], c[...], ((1,), (1,))))


def trailing_kernel(stack_ref, high_ref, low_ref, keep_ref, send_ref):
    n = stack_ref.shape[0] // 2
    breadth = high_ref.shape[1]
    tile = 256
    for k in range(breadth // tile):
        at = slice(k * tile, (k + 1) * tile)
        stacked = dot(stack_ref[...], high_ref[:, at], precision=None)
        total = stacked[:n] + stacked[n:] + dot(stack_ref[:n, :], low_ref[:, at], precision=None)
        keep_ref[:, at] = total[:n // 2]
        send_ref[:, at] = total[n // 2:]


def finish_kernel(grid, perm_ref, bbar_ref, factor_ref, inverse_t_ref, dbar_ref, rbar_ref, *refs):
    cores = grid.core[0]
    panel_refs, refs = refs[:cores], refs[cores:]
    products, (bbar_hbm, out_ref, rbar_out_ref, bbar_out, left_ref, sems) = refs[:-6], refs[-6:]
    me, my_col = lax.axis_index("row"), lax.axis_index("col")
    n, height, width = factor_ref.shape[0], grid.height, grid.width
    count = sems.shape[0]
    tile = bbar_ref.shape[1] // count
    left_ref[:, :n], left_ref[:, n:] = split(perm_ref[...].T)
    panels, copies = [], []

    def bbar_tile(k):
        at = slice(k * tile, (k + 1) * tile)
        high, low = split(jnp.concatenate([ref[:, at] for ref in panel_refs], axis=0))
        panels.append((high, low))
        update = dot(left_ref[...], jnp.concatenate([high, high], axis=0), precision=None)
        bbar_out[:, at] = bbar_ref[:, at] - (update + dot(left_ref[:, :n], low, precision=None))
        copies.append(pltpu.make_async_copy(bbar_out.at[:, pl.ds(k * tile, tile)], bbar_hbm.at[:, pl.ds(k * tile, tile)], sems.at[k]))
        copies[-1].start()

    product = unfold(add_pairs([ref[...] for ref in products]), n)
    bbar_tile(0)
    proj = phi(dot6(factor_ref[...].T, dbar_ref[...] - product))
    bbar_tile(1)
    if height % 8 == 0:
        weights = inverse_t_ref[pl.ds(pl.multiple_of(me * height, height), height), :]
    else:
        si, sj = iotas((height, n))
        weights = dot(hot(sj == me * height + si), inverse_t_ref[...])
    half = dot6(weights, proj + proj.T)
    bbar_tile(2)
    both = jnp.concatenate([inverse_t_ref[...], grid.permute_rows(inverse_t_ref, me)], axis=0)
    rows = dot6(half, both.T)
    for k in range(3, count):
        bbar_tile(k)
    rows_sym = rows[:, :n]
    high, low = split(rows[:, n:])
    for k, (panel_high, panel_low) in enumerate(panels):
        at = slice(k * tile, (k + 1) * tile)
        update = dot(high, panel_high, precision=None) + dot(low, panel_high, precision=None)
        rbar_out_ref[:, at] = rbar_ref[:, at] - (update + dot(high, panel_low, precision=None))
    si, sj = iotas((height, n))
    own_row = me * height + si
    rows_kernel = jnp.where(sj < own_row, rows_sym, jnp.where(sj == own_row, 0.5 * rows_sym, 0.0))
    out = rows_kernel[:, :width]
    for k in range(1, grid.cols):
        out = jnp.where(my_col == k, rows_kernel[:, k * width:(k + 1) * width], out)
    out_ref[...] = out
    for copy in copies:
        copy.wait()


def call(kernel, out_shape, scratch=(), limit=8 * MIB, flops=0, specs=None):
    return pl.pallas_call(
        kernel,
        out_shape=out_shape,
        scratch_shapes=list(scratch),
        compiler_params=pltpu.CompilerParams(vmem_limit_bytes=limit),
        cost_estimate=pl.CostEstimate(flops=flops, bytes_accessed=1, transcendentals=0),
        **({"in_specs": specs} if specs else {}),
    )


def after(value, *others):
    return lax.optimization_barrier((value, *others))[0]


def add_pairs(terms):
    while len(terms) > 1:
        terms = [a + b for a, b in zip(terms[::2], terms[1::2])]
    return terms[0]


def make_body(rows, cols):
    def row_parts(value, step):
        count, stride = step
        return [value] + [swap(value, "row", rows, d * stride) for d in range(count - 1, 0, -1)][::-1]

    def col_parts(value):
        return [value] + [swap(value, "col", cols, d) for d in range(1, cols)]

    def body(c_panel, cbar_in, factor, dbar_in, r_panel, rbar_in, b_block, bbar_in):
        n = factor.shape[0]
        depth, width = c_panel.shape
        height, breadth = r_panel.shape
        grid = Grid(rows, cols, height, width)

        cbar_parts, c_parts = col_parts(cbar_in.T), col_parts(c_panel.T)
        identity = call(identity_kernel, full((n, n)), flops=4 * 10 ** 9)()
        panel = jnp.concatenate(row_parts(r_panel, grid.z), axis=0)
        panel = jnp.concatenate(row_parts(panel, grid.x), axis=0)

        inverse_t, high, low = call(
            prepare_kernel,
            (full((n, n)), full((depth, breadth), BF16), full((depth, breadth), BF16)),
            [pltpu.VMEM((depth, breadth), F32), pltpu.SemaphoreType.DMA((8,))],
            limit=48 * MIB, flops=4 * 10 ** 9,
            specs=[pl.BlockSpec(memory_space=pltpu.VMEM)] * 2 + [pl.BlockSpec(memory_space=pltpu.HBM)],
        )(factor, identity, b_block)
        cbar_new_t, cbar_out_t, cbar_perm, stack = call(
            lambda *refs: cbar_kernel(grid, *refs),
            (full((n, depth)), full((width, depth)), full((n, depth)), full((2 * n, depth), BF16)),
            [pltpu.VMEM((n, depth), F32)], flops=10 ** 9,
        )(inverse_t, *cbar_parts)
        keep, send = call(trailing_kernel, (full((n // 2, breadth)),) * 2, flops=10 ** 9)(stack, high, low)
        product = call(
            lambda *refs: product_kernel(grid, *refs), full((8, (n // 16 + 1) * n)), [pltpu.VMEM((n, depth), F32)],
        )(after(cbar_new_t, send), *c_parts)
        product = add_pairs(row_parts(product, grid.core))
        summed = keep + swap(send, "row", rows, grid.core[1])
        product, summed = lax.optimization_barrier((product, summed))
        panel = after(panel, summed)
        product = add_pairs(row_parts(product, grid.z_near))
        product_parts = row_parts(product, grid.z_far)
        panel_parts = row_parts(panel, grid.core)
        product = add_pairs(product_parts)
        for count, stride in grid.order[1:]:
            own, *sends = summed.reshape(count, -1, breadth)
            got = [swap(value, "row", rows, d * stride) for d, value in list(enumerate(sends, 1))[::-1]][::-1]
            if stride == grid.x[1]:
                own = after(own, product)
            summed = add_pairs([own] + got[::-1])
            if stride == grid.x[1]:
                dbar_in = after(dbar_in, summed)
        vmem = pl.BlockSpec(memory_space=pltpu.VMEM)
        product_parts = row_parts(product, grid.x)
        bbar_out, kernel_out, rbar = pl.pallas_call(
            lambda *refs: finish_kernel(grid, *refs),
            in_specs=[vmem] * (6 + len(panel_parts) + len(product_parts)),
            out_specs=[pl.BlockSpec(memory_space=pltpu.HBM), vmem, vmem],
            out_shape=(full((depth, breadth)), full((height, width)), full((height, breadth))),
            scratch_shapes=[
                pltpu.VMEM((depth, breadth), F32), pltpu.VMEM((depth, 2 * n), BF16), pltpu.SemaphoreType.DMA((breadth // 256,))
            ],
            compiler_params=pltpu.CompilerParams(vmem_limit_bytes=16 * MIB),
            cost_estimate=pl.CostEstimate(flops=10 ** 9, bytes_accessed=1, transcendentals=0),
        )(cbar_perm, bbar_in, factor, inverse_t, dbar_in, rbar_in, *panel_parts, *product_parts)
        return (cbar_out_t.T, bbar_out, kernel_out, rbar - summed)

    return body


def solution(mesh):
    spec = P("row", "col")
    in_specs = (spec, spec, P(), P(), spec, spec, spec, spec)
    return jax.shard_map(
        make_body(mesh.shape["row"], mesh.shape["col"]),
        mesh=mesh, in_specs=in_specs, out_specs=(spec,) * 4, check_vma=False,
    )
```
